32 devices in a mesh: dp: 16 (over z, x, core), worker: 2 (over y).
Axes of the slice: x: 2, y: 2, z: 4, core: 2. Of those that a mesh axis runs over, the one named last changes fastest.
Arguments:
- acts: bfloat16 [16384, 4096], P('dp', 'worker'), may hold values from -6 to 6
- cotan: bfloat16 [16384, 4096], P('dp', 'worker'), may hold values from -0.15625 to 0.15625
- block_ids: int32 [32], P('dp'), may hold values from 0 to 7
- basis_in: bfloat16 [8, 512, 512], P('worker'), may hold values from -0.25 to 0.25
- basis_out: bfloat16 [8, 512, 512], replicated, may hold values from -0.25 to 0.25
- act_factor: float32 [8, 512, 512], P('worker'), may hold values from -0.0009375 to 1, as said below
- grad_factor: float32 [8, 512, 512], P('worker'), may hold values from -0.0009375 to 1, as said below
Outputs:
- precond: bfloat16 [4096, 4096], P('dp', 'worker')
- act_new: float32 [8, 512, 512], P('worker')
- grad_new: float32 [8, 512, 512], P('worker')
The draws below stay inside these ranges and needn't reach their ends.
Inputs may be any that keep to these rules, and one draw needn't show every extreme that they name: `act_factor`: each block is symmetric, and each diagonal entry exceeds the sum of magnitudes of the other entries of its row. `grad_factor`: each block is symmetric, and each diagonal entry exceeds the sum of magnitudes of the other entries of its row.
All inputs are finite; a program needn't handle non-finite values.
Results may differ from the reference program's by a relative error of at most 0.025.
Values may be sent and summed in bfloat16 or wider, within the bound.
No kernel may reach another device: no remote copies, remote signals or barrier semaphores. Data moves between devices by JAX's collectives and lax.ppermute only.
A program may use at most 128 MiB of HBM per device.

```python
import jax
import jax.numpy as jnp
from jax import lax

D = 4096
FB = 512
NB = 8
BLK = 128
POOL_BLK = 8
SAMP_BLK = 2
TOKENS = 16384
SAMPLES = 4096
N_DP = 16


def dominant_blocks(key):
    diag_key, outside_key = jax.random.split(key)
    diagonal = jax.random.uniform(diag_key, (NB, FB), jnp.float32, 0.5, 1.0)
    outside = jax.random.uniform(outside_key, (NB, FB, FB), jnp.float32, -1.0, 1.0)
    outside = (outside + jnp.swapaxes(outside, 1, 2)) * (0.24 / FB)
    identity = jnp.eye(FB, dtype=jnp.float32)
    return outside * (1.0 - identity) + identity * diagonal[:, :, None]


def draw_act_factor(key, part):
    key = jax.random.fold_in(key, 11)
    return dominant_blocks(key)


def draw_grad_factor(key, part):
    key = jax.random.fold_in(key, 23)
    return dominant_blocks(key)


def with_ends(values, rng, low, top_value):
    longest = values.shape.index(max(values.shape))
    spots = []
    for shift in (0, 1):
        where = [jax.random.randint(jax.random.fold_in(rng, axis), (), 0, length) for axis, length in enumerate(values.shape)]
        where[longest] = (where[longest] + shift) % values.shape[longest]
        spots.append(tuple(where))
    return values.at[spots[0]].set(low).at[spots[1]].set(top_value)


def spiked(result, rng, source, target, shards_of, factor):
    def block_of(position):
        return (jnp.arange(result.shape[position]) // (result.shape[position] // shards_of)).reshape((-1,) + (1,) * (result.ndim - 1 - position))

    one_side = jax.random.permutation(rng, shards_of)[block_of(target)]
    far = (block_of(target) + shards_of // 2) % shards_of
    return jnp.where((block_of(source) == one_side) | (block_of(source) == far), factor * result, result)


def block_scale(rng, extent, pieces, smallest, high):
    loudness, own = 1.0, jax.random.fold_in(rng, 6)
    for position, shards_of in pieces:
        steps = jnp.exp(jax.random.uniform(jax.random.fold_in(own, position), (shards_of,), jnp.float32, smallest / len(pieces), high / len(pieces)))
        loudness = loudness * jnp.repeat(steps, extent[position] // shards_of).reshape([-1 if axis == position else 1 for axis in range(len(extent))])
    return loudness


def gaussian(key, extent, deviation, bound, shards=(), kind=jnp.bfloat16):
    array = deviation * jax.random.normal(key, extent, jnp.float32)
    if shards:
        array = array * block_scale(key, extent, shards, -0.22, 0.18)
    return jnp.clip(array, -bound, bound).astype(kind)


def heavy_noise(own_key, dims, spread, bound, shards, heavy, kind=jnp.bfloat16):
    result = spread * jax.random.normal(own_key, dims, jnp.float32)
    if shards:
        result = result * block_scale(own_key, dims, shards, -0.22, 0.18)
    return jnp.clip(spiked(result, jax.random.fold_in(own_key, 3), *heavy), -bound, bound).astype(kind)


def setup_inputs(seed: int = 0) -> dict:
    arg_keys = jax.random.split(jax.random.key(seed), 8)
    acts = heavy_noise(arg_keys[0], (TOKENS, D), 1.0, 6.0, ((0, 16), (1, 2)), (0, 1, 16, 2.0))
    cotan = heavy_noise(arg_keys[1], (TOKENS, D), (TOKENS ** -0.5), 0.15625, ((0, 16), (1, 2)), (0, 1, 16, 2.0))
    block_ids = with_ends(jax.random.randint(arg_keys[2], (N_DP * SAMP_BLK,), 0, POOL_BLK), jax.random.fold_in(arg_keys[2], 1), 0, POOL_BLK - 1).astype(jnp.int32)
    basis_in = gaussian(arg_keys[3], (NB, FB, FB), FB ** -0.5, 0.25, ((0, 2),))
    basis_out = gaussian(arg_keys[4], (NB, FB, FB), FB ** -0.5, 0.25)
    act_factor = draw_act_factor(jax.random.fold_in(arg_keys[7], 71), 0)
    grad_factor = draw_grad_factor(jax.random.fold_in(arg_keys[7], 71), 0)
    return {"acts": acts, "cotan": cotan, "block_ids": block_ids, "basis_in": basis_in, "basis_out": basis_out, "act_factor": act_factor, "grad_factor": grad_factor}


DECAY_RATE = 0.75
DAMPING = 0.03


def rounded(values):
    return lax.optimization_barrier(values.astype(jnp.bfloat16)).astype(jnp.float32)


def reference(acts, cotan, block_ids, basis_in, basis_out, act_factor, grad_factor):
    highest = lax.Precision.HIGHEST
    pool_rows = POOL_BLK * BLK
    act_all = acts.reshape(N_DP, pool_rows, D)
    cot_all = cotan.reshape(N_DP, pool_rows, D)
    id_rows = block_ids.reshape(N_DP, SAMP_BLK)

    def replica(carry, inputs):
        grad_total, act_total, cot_total = carry
        act_rows, cot_rows, chosen = inputs
        term = jnp.dot(cot_rows.T, act_rows, preferred_element_type=jnp.float32)
        grad_total = grad_total + rounded(term)
        act_pick = act_rows.reshape(POOL_BLK, BLK, D)[chosen].reshape(SAMP_BLK * BLK, NB, FB).astype(jnp.float32)
        cot_pick = cot_rows.reshape(POOL_BLK, BLK, D)[chosen].reshape(SAMP_BLK * BLK, NB, FB).astype(jnp.float32)
        act_term = jnp.einsum('rbi,rbj->bij', act_pick, act_pick, precision=highest) / SAMPLES
        cot_term = jnp.einsum('rbi,rbj->bij', cot_pick, cot_pick, precision=highest) * (TOKENS / SAMPLES)
        return (grad_total, act_total + act_term, cot_total + cot_term), None

    start = (jnp.zeros((D, D), jnp.float32), jnp.zeros((NB, FB, FB), jnp.float32), jnp.zeros((NB, FB, FB), jnp.float32))
    (grad_total, act_total, cot_total), _ = lax.scan(replica, start, (act_all, cot_all, id_rows))
    act_new = DECAY_RATE * act_factor + (1.0 - DECAY_RATE) * act_total
    grad_new = DECAY_RATE * grad_factor + (1.0 - DECAY_RATE) * cot_total
    basis_act = basis_in.astype(jnp.float32)
    basis_cot = basis_out.astype(jnp.float32)
    eig_in = jnp.sum(basis_act * jnp.einsum('bij,bjk->bik', act_new, basis_act, precision=highest), axis=1)
    eig_out = jnp.sum(basis_cot * jnp.einsum('bij,bjk->bik', grad_new, basis_cot, precision=highest), axis=1)
    weight_grad = grad_total.astype(jnp.bfloat16).astype(jnp.float32).reshape(NB, FB, NB, FB)
    right_side = rounded(jnp.einsum('ribj,bjk->ribk', weight_grad, basis_act, precision=highest))
    inner_term = jnp.einsum('ira,irbk->iabk', basis_cot, right_side, precision=highest)
    scaled = rounded(inner_term / (eig_out[:, :, None, None] * eig_in[None, None, :, :] + DAMPING))
    upper_term = rounded(jnp.einsum('ira,iabk->irbk', basis_cot, scaled, precision=highest))
    precond = jnp.einsum('irbk,bjk->irbj', upper_term, basis_act, precision=highest)
    return precond.reshape(D, D).astype(jnp.bfloat16), act_new, grad_new
```

```python
import jax
import jax.numpy as jnp
from jax import lax
from jax.experimental import pallas as pl
from jax.experimental.pallas import tpu as pltpu
from jax.sharding import PartitionSpec as P

BLK = 128
QUARTER = 128
VMEM = 56 * 2**20
COL_CHUNKS = 2
DEPTH = 2


DECAY_RATE = 0.75
DAMPING = 0.03

BF16 = jnp.bfloat16
F32 = jnp.float32


def pack_upper(full):
    q = QUARTER
    first = full[:, :q, :]
    second = jnp.concatenate([full[:, q : 2 * q, q:], full[:, 3 * q :, 3 * q :]], axis=2)
    third = full[:, 2 * q : 3 * q, 2 * q :]
    third = jnp.concatenate([third[:, : q // 2], third[:, q // 2 :]], axis=2)
    return jnp.concatenate([first, second, third], axis=1)


def unpack_upper(packed):
    q = QUARTER
    tiles = {}
    for j in range(4):
        tiles[0, j] = packed[:q, j * q : (j + 1) * q]
    for j in range(1, 4):
        tiles[1, j] = packed[q : 2 * q, (j - 1) * q : j * q]
    tiles[3, 3] = packed[q : 2 * q, 3 * q :]
    third = jnp.concatenate([packed[2 * q :, : 2 * q], packed[2 * q :, 2 * q :]], axis=0)
    tiles[2, 2], tiles[2, 3] = third[:, :q], third[:, q:]
    return [[tiles[i, j] if j >= i else tiles[j, i].T for j in range(4)] for i in range(4)]


def factor_kernel(start_ref, *refs):
    del start_ref
    for packed, factor, basis, new, eig in zip(refs[0:2], refs[2:4], refs[4:6], refs[6:8], refs[8:10]):
        rows = unpack_upper(packed[0].astype(F32))
        q = QUARTER
        for i in range(4):
            for j in range(4):
                at = (0, pl.ds(i * q, q), pl.ds(j * q, q))
                new[at] = DECAY_RATE * factor[at] + (1.0 - DECAY_RATE) * rows[i][j]
        vectors = basis[0]
        rest = new[0]
        product = 0.0
        for _ in range(3):
            part = rest.astype(BF16)
            rest = rest - part.astype(F32)
            product = product + jnp.dot(part, vectors, preferred_element_type=F32)
        eig[0] = jnp.sum(vectors.astype(F32) * product, axis=0, keepdims=True)


def update_factors(packed, factors, basis_in, basis_out, first_block):
    blocks, size, _ = basis_in.shape
    packed_rows = packed[0].shape[1]

    def local(b, start):
        return (b, 0, 0)

    square = pl.BlockSpec((1, size, size), local)
    narrow = pl.BlockSpec((1, packed_rows, size), local)
    line = pl.BlockSpec((1, 1, size), local)
    return pl.pallas_call(
        factor_kernel,
        grid_spec=pltpu.PrefetchScalarGridSpec(
            num_scalar_prefetch=1,
            grid=(blocks,),
            in_specs=[narrow, narrow, square, square, square]
            + [pl.BlockSpec((1, size, size), lambda b, start: (start[0] + b, 0, 0))],
            out_specs=[square, square, line, line],
        ),
        out_shape=[jax.ShapeDtypeStruct((blocks, size, size), F32)] * 2
        + [jax.ShapeDtypeStruct((blocks, 1, size), F32)] * 2,
        compiler_params=pltpu.CompilerParams(vmem_limit_bytes=VMEM),
        cost_estimate=pl.CostEstimate(
            flops=blocks * 12 * size**3, bytes_accessed=blocks * 19 * size**2, transcendentals=0
        ),
    )(first_block, *packed, *factors, basis_in, basis_out)


def tail_kernel(place_ref, *refs):
    parts, (basis, outer, eig_in, eig_out, out, whole) = refs[:-6], refs[-6:]
    sharers = len(parts)
    rows = parts[0].shape[0]
    me = place_ref[1]
    for step, part in enumerate(parts):
        spot = lax.rem(me - step + sharers, sharers)
        whole[pl.ds(pl.multiple_of(spot * rows, rows), rows), :] = part[...]
    right = jnp.dot(whole[...], basis[0], preferred_element_type=F32).astype(BF16)
    inner = lax.dot_general(outer[0], right, (((0,), (0,)), ((), ())), preferred_element_type=F32)
    scaled = (inner / (eig_out[...] * eig_in[0] + DAMPING)).astype(BF16)
    mine = outer[0, pl.ds(pl.multiple_of(me * rows, rows), rows), :]
    upper = jnp.dot(mine, scaled, preferred_element_type=F32).astype(BF16)
    out[...] = lax.dot_general(
        upper, basis[0], (((1,), (1,)), ((), ())), preferred_element_type=F32
    ).astype(BF16)


def tail(place, parts, basis_in, basis_out, eig_in, eig_out):
    blocks, size, _ = basis_in.shape
    rows, width = parts[0].shape
    strip = pl.BlockSpec((rows, size), lambda b, place: (0, b))
    return pl.pallas_call(
        tail_kernel,
        grid_spec=pltpu.PrefetchScalarGridSpec(
            num_scalar_prefetch=1,
            grid=(blocks,),
            in_specs=[strip] * len(parts)
            + [
                pl.BlockSpec((1, size, size), lambda b, place: (b, 0, 0)),
                pl.BlockSpec((1, size, size), lambda b, place: (place[0], 0, 0)),
                pl.BlockSpec((1, 1, size), lambda b, place: (b, 0, 0)),
                pl.BlockSpec((size, 1), lambda b, place: (0, 0)),
            ],
            out_specs=strip,
            scratch_shapes=[pltpu.VMEM((size, size), BF16)],
        ),
        out_shape=jax.ShapeDtypeStruct((rows, width), BF16),
        compiler_params=pltpu.CompilerParams(vmem_limit_bytes=VMEM),
        cost_estimate=pl.CostEstimate(
            flops=blocks * 6 * size**3, bytes_accessed=4 * blocks * size**2, transcendentals=0
        ),
    )(place, *parts, basis_in, basis_out, eig_in, eig_out)


def product_kernel(*refs):
    left, right, outs, turned = refs[:2], refs[2:4], refs[4:-1], refs[-1]
    step = pl.program_id(0)
    tokens = left[0].shape[0]

    @pl.when(step == 0)
    def _():
        for i in range(2):
            turned[:, i * tokens : (i + 1) * tokens] = left[i][...].T

    total = jnp.dot(turned[:, :tokens], right[0][...], preferred_element_type=F32)
    total = total + jnp.dot(turned[:, tokens:], right[1][...], preferred_element_type=F32)
    each = pl.num_programs(0) // len(outs)
    for n, out in enumerate(outs):

        @pl.when(step // each == n)
        def _(out=out):
            out[...] = total.astype(BF16)


def products(pieces, rows, chunks):
    tokens, width = rows[0].shape
    n_rows = pieces[0].shape[1]
    tile = 512
    each = width // chunks // tile
    whole = pl.BlockSpec((tokens, n_rows), lambda i: (0, 0))
    strip = pl.BlockSpec((tokens, tile), lambda i: (0, i))
    return pl.pallas_call(
        product_kernel,
        grid=(width // tile,),
        in_specs=[whole, whole, strip, strip],
        out_specs=[
            pl.BlockSpec((n_rows, tile), lambda i, n=n: (0, jnp.clip(i - n * each, 0, each - 1)))
            for n in range(chunks)
        ],
        out_shape=[jax.ShapeDtypeStruct((n_rows, width // chunks), BF16)] * chunks,
        scratch_shapes=[pltpu.VMEM((n_rows, 2 * tokens), BF16)],
        compiler_params=pltpu.CompilerParams(vmem_limit_bytes=VMEM),
        cost_estimate=pl.CostEstimate(
            flops=4 * tokens * n_rows * width, bytes_accessed=4 * tokens * width, transcendentals=0
        ),
    )(*pieces, *rows)


def per_device(acts, cotan, block_ids, basis_in, basis_out, act_factor, grad_factor):
    n_dp = lax.axis_size("dp")
    n_worker = lax.axis_size("worker")
    d = lax.axis_index("dp")
    w = lax.axis_index("worker")
    core, x = d % 2, (d // 2) % 2
    n_z = n_dp // 4
    pool_rows, width = acts.shape
    local_blocks, block_size, _ = basis_in.shape
    model_width = basis_out.shape[0] * block_size
    samples = block_ids.shape[0] * BLK * n_dp
    tokens = pool_rows * n_dp
    rows_dev = model_width // n_dp
    z_per_worker = n_z // n_worker
    cols = width // COL_CHUNKS if width >= 1024 else width
    both = ("dp", "worker")

    def swap_core(v):
        return lax.ppermute(v, "dp", [(i, i ^ 1) for i in range(n_dp)])

    def swap_x(v):
        return lax.ppermute(v, "dp", [(i, i ^ 2) for i in range(n_dp)])

    def from_worker(v, step, flip):
        return lax.ppermute(
            v,
            both,
            [
                ((i ^ flip) * n_worker + (j + step) % n_worker, i * n_worker + j)
                for i in range(n_dp)
                for j in range(n_worker)
            ],
        )

    def place(owner, j):
        return owner * z_per_worker + (j if owner < n_worker // 2 else z_per_worker - 1 - j)

    z = d // 4
    starts = list(range(0, width, cols))
    shards = [(step, j) for j in range(z_per_worker) for step in range(n_worker)]

    def hops_of(step, j):
        ends = [place((i + step) % n_worker, j) for i in range(n_worker)]
        hops = []
        for hop in range(1, n_z):
            moves = []
            for i in range(n_worker):
                if hop <= ends[i]:
                    moves.append((i, hop - 1, hop))
                if hop <= n_z - 1 - ends[i]:
                    moves.append((i, n_z - hop, n_z - hop - 1))
            if moves:
                hops.append(moves)
        return hops

    def hop(v, moves):
        return lax.ppermute(
            v,
            both,
            [((a * 4 + r) * n_worker + i, (b * 4 + r) * n_worker + i) for i, a, b in moves for r in range(4)],
        )

    def piece(rows, j, at, flip):
        part = jnp.where(w < n_worker // 2, j, z_per_worker - 1 - j)
        x_to = x if at else 1 - x
        core_to = 1 - core if flip else core
        return lax.dynamic_slice_in_dim(rows, ((part * 2 + x_to) * 2 + core_to) * rows_dev, rows_dev, 1)

    def pick(v):
        return jnp.take(v.reshape(pool_rows // BLK, BLK, width), block_ids, axis=0).reshape(-1, width)

    y_items = [(step, j, at, flip) for step, j in shards if step for at in range(2) for flip in range(2)]
    y_stage = {item: max(0, at - 1) for at, item in enumerate(y_items)}
    x_items = [(step, j, n) for step, j in shards for n in range(len(starts))]
    x_stage, z_stage, mine_stage, other_stage, busy = {}, {}, {}, {}, set()
    clock = 0
    for step, j, n in x_items:
        ready = y_stage[step, j, 0, 1] + DEPTH if step else 0
        clock = max(clock, ready) + 1
        x_stage[step, j, n] = clock
        if n == 0:
            other_stage[step, j] = clock - 1
            mine_stage[step, j] = max(clock + 1, y_stage[step, j, 1, 1] + DEPTH if step else 0)
    for step, j, n in x_items:
        clock = max(x_stage[step, j, n] + DEPTH, mine_stage[step, j] + 1)
        for at, moves in enumerate(hops_of(step, j)):
            while any((clock, move) in busy for move in moves):
                clock += 1
            busy.update((clock, move) for move in moves)
            z_stage[step, j, n, at] = clock
            clock += DEPTH
    last = max(z_stage.values()) + DEPTH - 1

    groups = [[i * 4 + r for i in range(n_z)] for r in range(4)]
    is_act = core == 0
    env = {"acts": acts, "cotan": cotan}
    pending = {}

    def want(stage):
        keys = {(item[1], item[2], item[3]) for item, when in y_stage.items() if when == stage}
        for j in range(z_per_worker):
            if stage == min(j, 1):
                keys |= {(j, at, flip) for at in range(2) for flip in range(2)}
        return sorted(keys)

    for j, at, flip in want(0):
        env["p", j, at, flip] = piece(cotan, j, at, flip)
    for n in range(len(starts)):
        env["sum", n] = jnp.zeros((rows_dev, cols), BF16)
    env["act_pick"], env["cot_pick"] = pick(acts), pick(cotan)
    reduced = gathered = None
    for stage in range(last + 1):
        keys = sorted(env, key=str)
        env = dict(zip(keys, lax.optimization_barrier(tuple(env[k] for k in keys))))
        soon, late = {}, {}
        if stage == 0:
            soon["acts_sib"] = swap_core(env["acts"])
            soon["theirs"] = swap_core(jnp.where(is_act, env["cot_pick"], env["act_pick"]))
            soon["ours"] = jnp.where(is_act, env.pop("act_pick"), env.pop("cot_pick"))
        for item, when in y_stage.items():
            if when == stage:
                step, j, at, flip = item
                late["c", step, j, at, flip] = from_worker(env["p", j, at, flip], step, flip)
        for step, j, n in x_items:
            if x_stage[step, j, n] == stage:
                late["got", step, j, n] = swap_x(env.pop(("out", step, j, n)))
        for (step, j, n, at), when in z_stage.items():
            if when == stage:
                late["hop", step, j, n] = hop(env["acc", step, j, n], hops_of(step, j)[at])
        for j in range(z_per_worker):
            if stage == min(j, 1):
                for at in range(2):
                    soon["c", 0, j, at, 0] = env["p", j, at, 0]
                    soon["c", 0, j, at, 1] = swap_core(env["p", j, at, 1])
        for key in want(stage + 1):
            if ("p", *key) not in env:
                soon[("p", *key)] = piece(env["cotan"], *key)

        ready = {**env, **soon} if stage == 0 else env
        rows = (ready["acts"], ready["acts_sib"])
        for step, j in shards:
            for at, when, name in ((0, other_stage, "out"), (1, mine_stage, "mine")):
                if when[step, j] == stage:
                    pair = [ready["c", step, j, at, flip] for flip in range(2)]
                    for n, out in enumerate(products(pair, rows, len(starts))):
                        soon[name, step, j, n] = out

        if stage == 1:
            sample = jnp.concatenate([env.pop("ours"), env.pop("theirs")], axis=0)
            sample = sample.reshape(-1, local_blocks, block_size)
            scale = jnp.where(is_act, 1.0 / samples, tokens / samples)
            term = jnp.einsum("rbi,rbj->bij", sample, sample, preferred_element_type=F32) * scale
            packed = pack_upper(term.astype(BF16)).reshape(2, -1, block_size)
            soon["half"] = lax.dynamic_index_in_dim(packed, x, 0, keepdims=False)
            soon["away"] = lax.dynamic_index_in_dim(packed, 1 - x, 0, keepdims=False)
        if stage == 2:
            late["back"] = swap_x(env.pop("away"))
        if stage == 4:
            half = (env.pop("half").astype(F32) + env.pop("back").astype(F32)).astype(BF16)
            reduced = lax.psum_scatter(half, "dp", axis_index_groups=groups, tiled=True)
        if stage == 6:
            soon["reduced"] = reduced
        if stage == 7:
            gathered = lax.all_gather(env.pop("reduced"), "dp", axis_index_groups=groups, tiled=True)
        if stage == last - 4:
            soon["half"] = gathered
        if stage == last - 3:
            late["back"] = swap_x(env["half"])
        if stage == last - 1:
            half, back = env.pop("half"), env.pop("back")
            packed = jnp.where(x == 0, jnp.stack([half, back]), jnp.stack([back, half]))
            packed = packed.reshape(local_blocks, -1, block_size)
            packed_sib = swap_core(packed)
            soon["packed_act"] = jnp.where(is_act, packed, packed_sib)
            soon["packed_cot"] = jnp.where(is_act, packed_sib, packed)
        if stage == last:
            act_new, grad_new, eig_in, eig_local = update_factors(
                (env.pop("packed_act"), env.pop("packed_cot")),
                (act_factor, grad_factor),
                basis_in,
                basis_out,
                jnp.reshape(w * local_blocks, (1,)),
            )

        env.update(soon)
        env.update(pending)
        pending = late
        for step, j, n in x_items:
            mine, got, acc = ("mine", step, j, n), ("got", step, j, n), ("acc", step, j, n)
            if mine in env and got in env:
                env[acc] = (env.pop(mine).astype(F32) + env.pop(got).astype(F32)).astype(BF16)
            if ("hop", step, j, n) in env:
                total = (env[acc].astype(F32) + env.pop(("hop", step, j, n)).astype(F32)).astype(BF16)
                env[acc] = total
                if stage == z_stage[step, j, n, len(hops_of(step, j)) - 1] + DEPTH - 1:
                    ends = jnp.array([place((i + step) % n_worker, j) for i in range(n_worker)], jnp.int32)
                    env["sum", n] = jnp.where(ends[w] == z, env.pop(acc), env["sum", n])
    summed = jnp.concatenate([env["sum", n] for n in range(len(starts))], axis=1)

    my_start = d * rows_dev
    block = my_start // block_size
    eig_block = jnp.zeros((block_size,), F32)
    for step in range(n_worker):
        held = eig_local if step == 0 else from_worker(eig_local, step, 0)
        row = lax.dynamic_index_in_dim(held, block % local_blocks, 0, keepdims=False)[0]
        owner = (w + step) % n_worker
        eig_block = jnp.where(owner == block // local_blocks, row, eig_block)

    sharers = block_size // rows_dev
    parts = [summed]
    for step in range(1, sharers):
        pairs = [(i, i // sharers * sharers + (i + step) % sharers) for i in range(n_dp)]
        parts.append(lax.ppermute(summed, "dp", pairs))
    spot = jnp.stack([block, d % sharers]).astype(jnp.int32)
    precond = tail(spot, parts, basis_in, basis_out, eig_in, eig_block[:, None])
    return precond, act_new, grad_new


def solution(mesh):
    return jax.shard_map(
        per_device,
        mesh=mesh,
        in_specs=(
            P("dp", "worker"),
            P("dp", "worker"),
            P("dp"),
            P("worker", None, None),
            P(),
            P("worker", None, None),
            P("worker", None, None),
        ),
        out_specs=(P("dp", "worker"), P("worker", None, None), P("worker", None, None)),
        check_vma=False,
    )
```

```python
import functools

import jax
import jax.numpy as jnp
from jax import lax
from jax.experimental import pallas as pl
from jax.experimental.pallas import tpu as pltpu
from jax.sharding import PartitionSpec as P

BLK = 128
QUARTER = 128
VMEM = 56 * 2**20
COL_CHUNKS = 2
DEPTH = 2


DECAY_RATE = 0.75
DAMPING = 0.03

BF16 = jnp.bfloat16
F32 = jnp.float32


def pick_kernel(n_picks, which_ref, acts, cotan, ours, theirs):
    is_act = which_ref[n_picks] == 0
    ours[...] = jnp.where(is_act, acts[...], cotan[...])
    theirs[...] = jnp.where(is_act, cotan[...], acts[...])


def pick(acts, cotan, block_ids, core):
    n_picks, width = block_ids.shape[0], acts.shape[1]
    chosen = pl.BlockSpec((BLK, width), lambda i, which: (which[i], 0))
    out = pl.BlockSpec((BLK, width), lambda i, which: (i, 0))
    return pl.pallas_call(
        functools.partial(pick_kernel, n_picks),
        grid_spec=pltpu.PrefetchScalarGridSpec(
            num_scalar_prefetch=1, grid=(n_picks,), in_specs=[chosen] * 2, out_specs=[out] * 2
        ),
        out_shape=[jax.ShapeDtypeStruct((n_picks * BLK, width), BF16)] * 2,
        compiler_params=pltpu.CompilerParams(vmem_limit_bytes=VMEM),
        cost_estimate=pl.CostEstimate(
            flops=0, bytes_accessed=8 * n_picks * BLK * width, transcendentals=0
        ),
    )(jnp.concatenate([block_ids, jnp.reshape(core, (1,))]).astype(jnp.int32), acts, cotan)


def pack_upper(full):
    q = QUARTER
    second = jnp.concatenate([full[q : 2 * q, q:], full[3 * q :, 3 * q :]], axis=1)
    third = full[2 * q : 3 * q, 2 * q :]
    third = jnp.concatenate([third[: q // 2], third[q // 2 :]], axis=1)
    return jnp.concatenate([full[:q], second, third], axis=0)


def term_kernel(scales, place_ref, ours, theirs, keep, away):
    total = 0.0
    for rows in (ours[...], theirs[...]):
        total = total + lax.dot_general(
            rows, rows, (((0,), (0,)), ((), ())), preferred_element_type=F32
        )
    scale = jnp.where(place_ref[0] == 0, scales[0], scales[1]).astype(F32)
    packed = pack_upper(total * scale)
    half = packed.shape[0] // 2
    low = place_ref[1] == 0
    keep[0] = jnp.where(low, packed[:half], packed[half:]).astype(BF16)
    away[0] = jnp.where(low, packed[half:], packed[:half]).astype(BF16)


def terms(place, ours, theirs, size, scales):
    rows, width = ours.shape
    blocks, half = width // size, 5 * QUARTER // 4
    strip = pl.BlockSpec((rows, size), lambda b, place: (0, b))
    out = pl.BlockSpec((1, half, size), lambda b, place: (b, 0, 0))
    return pl.pallas_call(
        functools.partial(term_kernel, scales),
        grid_spec=pltpu.PrefetchScalarGridSpec(
            num_scalar_prefetch=1, grid=(blocks,), in_specs=[strip] * 2, out_specs=[out] * 2
        ),
        out_shape=[jax.ShapeDtypeStruct((blocks, half, size), BF16)] * 2,
        compiler_params=pltpu.CompilerParams(vmem_limit_bytes=VMEM),
        cost_estimate=pl.CostEstimate(
            flops=4 * rows * width * size, bytes_accessed=8 * rows * width, transcendentals=0
        ),
    )(place, ours, theirs)


def unpack_upper(packed):
    q = QUARTER
    tiles = {}
    for j in range(4):
        tiles[0, j] = packed[:q, j * q : (j + 1) * q]
    for j in range(1, 4):
        tiles[1, j] = packed[q : 2 * q, (j - 1) * q : j * q]
    tiles[3, 3] = packed[q : 2 * q, 3 * q :]
    third = jnp.concatenate([packed[2 * q :, : 2 * q], packed[2 * q :, 2 * q :]], axis=0)
    tiles[2, 2], tiles[2, 3] = third[:, :q], third[:, q:]
    return [[tiles[i, j] if j >= i else tiles[j, i].T for j in range(4)] for i in range(4)]


def factor_kernel(place_ref, keep, back, keep_sib, back_sib, *refs):
    low = place_ref[2] == 0
    for kind, (factor, basis, new, eig) in enumerate(zip(refs[0:2], refs[2:4], refs[4:6], refs[6:8])):
        here = place_ref[1] == kind
        kept = jnp.where(here, keep[0], keep_sib[0])
        came = jnp.where(here, back[0], back_sib[0])
        halves = [jnp.where(low, kept, came), jnp.where(low, came, kept)]
        rows = unpack_upper(jnp.concatenate(halves, axis=0).astype(F32))
        q = QUARTER
        for i in range(4):
            for j in range(4):
                at = (0, pl.ds(i * q, q), pl.ds(j * q, q))
                new[at] = DECAY_RATE * factor[at] + (1.0 - DECAY_RATE) * rows[i][j]
        vectors = basis[0]
        rest = new[0]
        product = 0.0
        for _ in range(3):
            part = rest.astype(BF16)
            rest = rest - part.astype(F32)
            product = product + jnp.dot(part, vectors, preferred_element_type=F32)
        eig[0] = jnp.sum(vectors.astype(F32) * product, axis=0, keepdims=True)


def update_factors(place, halves, factors, basis_in, basis_out):
    blocks, size, _ = basis_in.shape

    def local(b, place):
        return (b, 0, 0)

    square = pl.BlockSpec((1, size, size), local)
    narrow = pl.BlockSpec((1, halves[0].shape[1], size), local)
    line = pl.BlockSpec((1, 1, size), local)
    return pl.pallas_call(
        factor_kernel,
        grid_spec=pltpu.PrefetchScalarGridSpec(
            num_scalar_prefetch=1,
            grid=(blocks,),
            in_specs=[narrow] * 4
            + [square] * 3
            + [pl.BlockSpec((1, size, size), lambda b, place: (place[0] + b, 0, 0))],
            out_specs=[square, square, line, line],
        ),
        out_shape=[jax.ShapeDtypeStruct((blocks, size, size), F32)] * 2
        + [jax.ShapeDtypeStruct((blocks, 1, size), F32)] * 2,
        compiler_params=pltpu.CompilerParams(vmem_limit_bytes=VMEM),
        cost_estimate=pl.CostEstimate(
            flops=blocks * 12 * size**3, bytes_accessed=blocks * 19 * size**2, transcendentals=0
        ),
    )(place, *halves, *factors, basis_in, basis_out)


def tail_kernel(n_parts, place_ref, *refs):
    parts, (basis, outer, eig_in, eig_out) = refs[:n_parts], refs[n_parts : n_parts + 4]
    out, whole = refs[-2:]
    sharers = len(parts)
    rows = parts[0].shape[0]
    me = place_ref[1]
    for step, part in enumerate(parts):
        spot = lax.rem(me - step + sharers, sharers)
        whole[pl.ds(pl.multiple_of(spot * rows, rows), rows), :] = part[...]
    right = jnp.dot(whole[...], basis[0], preferred_element_type=F32).astype(BF16)
    inner = lax.dot_general(outer[0], right, (((0,), (0,)), ((), ())), preferred_element_type=F32)
    scaled = (inner / (eig_out[...] * eig_in[0] + DAMPING)).astype(BF16)
    mine = outer[0, pl.ds(pl.multiple_of(me * rows, rows), rows), :]
    upper = jnp.dot(mine, scaled, preferred_element_type=F32).astype(BF16)
    out[...] = lax.dot_general(
        upper, basis[0], (((1,), (1,)), ((), ())), preferred_element_type=F32
    ).astype(BF16)


def tail(place, parts, basis_in, basis_out, eig_in, eig_out, chunk, filled):
    blocks, size, _ = basis_in.shape
    rows, cols = parts[0].shape
    each = cols // size
    strip = pl.BlockSpec((rows, size), lambda b, place: (0, b))
    in_specs = [strip] * len(parts) + [
        pl.BlockSpec((1, size, size), lambda b, place: (chunk * each + b, 0, 0)),
        pl.BlockSpec((1, size, size), lambda b, place: (place[0], 0, 0)),
        pl.BlockSpec((1, 1, size), lambda b, place: (chunk * each + b, 0, 0)),
        pl.BlockSpec((size, 1), lambda b, place: (0, 0)),
    ]
    args = [place, *parts, basis_in, basis_out, eig_in, eig_out]
    aliases = {}
    if filled is not None:
        in_specs.append(pl.BlockSpec(memory_space=pl.ANY))
        aliases = {len(args): 0}
        args.append(filled)
    return pl.pallas_call(
        functools.partial(tail_kernel, len(parts)),
        grid_spec=pltpu.PrefetchScalarGridSpec(
            num_scalar_prefetch=1,
            grid=(each,),
            in_specs=in_specs,
            out_specs=pl.BlockSpec((rows, size), lambda b, place: (0, chunk * each + b)),
            scratch_shapes=[pltpu.VMEM((size, size), BF16)],
        ),
        out_shape=jax.ShapeDtypeStruct((rows, blocks * size), BF16),
        input_output_aliases=aliases,
        compiler_params=pltpu.CompilerParams(vmem_limit_bytes=VMEM),
        cost_estimate=pl.CostEstimate(
            flops=each * 6 * size**3, bytes_accessed=4 * each * size**2, transcendentals=0
        ),
    )(*args)


def turn_kernel(which_ref, block, *outs):
    del which_ref
    for n, out in enumerate(outs):

        @pl.when(pl.program_id(0) == n)
        def _(out=out):
            out[...] = block[...].T


def turned(rows, which, n_rows):
    tokens, _ = rows.shape
    return pl.pallas_call(
        turn_kernel,
        grid_spec=pltpu.PrefetchScalarGridSpec(
            num_scalar_prefetch=1,
            grid=(len(which),),
            in_specs=[pl.BlockSpec((tokens, n_rows), lambda i, which: (0, which[i]))],
            out_specs=[pl.BlockSpec((n_rows, tokens), lambda i, which: (0, 0))] * len(which),
        ),
        out_shape=[jax.ShapeDtypeStruct((n_rows, tokens), BF16)] * len(which),
        compiler_params=pltpu.CompilerParams(vmem_limit_bytes=VMEM),
        cost_estimate=pl.CostEstimate(
            flops=0, bytes_accessed=4 * len(which) * tokens * n_rows, transcendentals=0
        ),
    )(jnp.stack(which).astype(jnp.int32), rows)


def product_kernel(n_pairs, *refs):
    pieces, right, outs, left = refs[: 2 * n_pairs], refs[2 * n_pairs : 2 * n_pairs + 2], refs[2 * n_pairs + 2 : -1], refs[-1]
    step = pl.program_id(0)
    rows, tokens = pieces[0].shape

    @pl.when(step == 0)
    def _():
        for n, piece in enumerate(pieces):
            left[n // 2 * rows : (n // 2 + 1) * rows, n % 2 * tokens : (n % 2 + 1) * tokens] = piece[...]

    total = jnp.dot(left[:, :tokens], right[0][...], preferred_element_type=F32)
    total = total + jnp.dot(left[:, tokens:], right[1][...], preferred_element_type=F32)
    chunks = len(outs) // n_pairs
    each = pl.num_programs(0) // chunks
    for n in range(chunks):

        @pl.when(step // each == n)
        def _(n=n):
            for m in range(n_pairs):
                outs[m * chunks + n][...] = total[m * rows : (m + 1) * rows].astype(BF16)


def products(pairs, rows, chunks):
    tokens, width = rows[0].shape
    n_rows = pairs[0][0].shape[0]
    tile = 512
    each = width // chunks // tile
    whole = pl.BlockSpec((n_rows, tokens), lambda i: (0, 0))
    strip = pl.BlockSpec((tokens, tile), lambda i: (0, i))
    outs = pl.pallas_call(
        functools.partial(product_kernel, len(pairs)),
        grid=(width // tile,),
        in_specs=[whole] * (2 * len(pairs)) + [strip] * 2,
        out_specs=[
            pl.BlockSpec((n_rows, tile), lambda i, n=n: (0, jnp.clip(i - n * each, 0, each - 1)))
            for _ in pairs
            for n in range(chunks)
        ],
        out_shape=[jax.ShapeDtypeStruct((n_rows, width // chunks), BF16)] * (chunks * len(pairs)),
        scratch_shapes=[pltpu.VMEM((len(pairs) * n_rows, 2 * tokens), BF16)],
        compiler_params=pltpu.CompilerParams(vmem_limit_bytes=VMEM),
        cost_estimate=pl.CostEstimate(
            flops=4 * len(pairs) * tokens * n_rows * width,
            bytes_accessed=4 * tokens * width,
            transcendentals=0,
        ),
    )(*[piece for pair in pairs for piece in pair], *rows)
    return [outs[m * chunks : (m + 1) * chunks] for m in range(len(pairs))]


def per_device(acts, cotan, block_ids, basis_in, basis_out, act_factor, grad_factor):
    n_dp = lax.axis_size("dp")
    n_worker = lax.axis_size("worker")
    d = lax.axis_index("dp")
    w = lax.axis_index("worker")
    core, x = d % 2, (d // 2) % 2
    n_z = n_dp // 4
    pool_rows, width = acts.shape
    local_blocks, block_size, _ = basis_in.shape
    model_width = basis_out.shape[0] * block_size
    samples = block_ids.shape[0] * BLK * n_dp
    tokens = pool_rows * n_dp
    rows_dev = model_width // n_dp
    z_per_worker = n_z // n_worker
    cols = width // COL_CHUNKS if width >= 1024 else width
    both = ("dp", "worker")

    def swap_core(v):
        return lax.ppermute(v, "dp", [(i, i ^ 1) for i in range(n_dp)])

    def swap_x(v):
        return lax.ppermute(v, "dp", [(i, i ^ 2) for i in range(n_dp)])

    def from_worker(v, step, flip):
        return lax.ppermute(
            v,
            both,
            [
                ((i ^ flip) * n_worker + (j + step) % n_worker, i * n_worker + j)
                for i in range(n_dp)
                for j in range(n_worker)
            ],
        )

    def place(owner, j):
        return owner * z_per_worker + (j if owner < n_worker // 2 else z_per_worker - 1 - j)

    z = d // 4
    starts = list(range(0, width, cols))
    shards = [(step, j) for j in range(z_per_worker) for step in range(n_worker)]

    def hops_of(step, j):
        hops = []
        size = 1
        while size < n_z:
            moves = []
            for i in range(n_worker):
                end = place((i + step) % n_worker, j)
                for low in range(0, n_z, 2 * size):
                    heads = [min(max(end, at), at + size - 1) for at in (low, low + size)]
                    to = min(max(end, low), low + 2 * size - 1)
                    moves.append((i, sum(heads) - to, to))
            hops.append(moves)
            size *= 2
        return hops

    def links(moves):
        found = set()
        for i, a, b in moves:
            ahead = 1 if b > a else -1
            found.update((i, at, at + ahead) for at in range(a, b, ahead))
        return found

    def swap_z(v, far):
        return lax.ppermute(v, "dp", [(i, (i + 4 * far) % n_dp) for i in range(n_dp)])

    def hop(v, moves):
        return lax.ppermute(
            v,
            both,
            [((a * 4 + r) * n_worker + i, (b * 4 + r) * n_worker + i) for i, a, b in moves for r in range(4)],
        )

    def piece(j, at, flip):
        part = jnp.where(w < n_worker // 2, j, z_per_worker - 1 - j)
        x_to = x if at else 1 - x
        core_to = 1 - core if flip else core
        return (part * 2 + x_to) * 2 + core_to

    y_items = [(step, j, at, flip) for step, j in shards if step for at in range(2) for flip in range(2)]
    y_stage = {item: max(0, at - 1) for at, item in enumerate(y_items)}
    x_items = [(step, j, n) for step, j in shards for n in range(len(starts))]
    x_stage, z_stage, product_stage, busy = {}, {}, {}, set()
    clock = 0
    for step, j, n in x_items:
        ready = y_stage[step, j, 0, 1] + DEPTH if step else 0
        clock = max(clock, ready) + 1
        x_stage[step, j, n] = clock
        if n == 0:
            product_stage[step, j, 0] = clock - 1
            product_stage[step, j, 1] = max(clock + 1, y_stage[step, j, 1, 1] + DEPTH if step else 2)
            if step == 0 and j > 0:
                product_stage[step, j, 0] = product_stage[step, j, 1] = 3
    for step, j, n in x_items:
        clock = max(x_stage[step, j, n] + DEPTH, product_stage[step, j, 1] + 1)
        for at, moves in enumerate(hops_of(step, j)):
            while any((clock, link) in busy for link in links(moves)):
                clock += 1
            busy.update((clock, link) for link in links(moves))
            z_stage[step, j, n, at] = clock
            clock += DEPTH
    last = max(z_stage.values()) + DEPTH - 1

    my_start = d * rows_dev
    block = my_start // block_size
    flags = jnp.stack([w * local_blocks, core, x]).astype(jnp.int32)
    env = {"acts": acts, "cotan": cotan}
    pending = {}
    first = [(0, 0, 1), (0, 0, 0)]
    others = [(j, at, flip) for j in range(z_per_worker) for at in range(2) for flip in range(2)]
    others = [key for key in others if key not in first]
    done = {}
    for stage in range(last + 1):
        if stage:
            keys = sorted(env, key=str)
            env = dict(zip(keys, lax.optimization_barrier(tuple(env[k] for k in keys))))
        soon, late = {}, {}
        if stage == 0:
            soon["acts_sib"] = swap_core(acts)
            for key, part in zip(first, turned(cotan, [piece(*key) for key in first], rows_dev)):
                env["p", *key] = part
            for key, part in zip(others, turned(cotan, [piece(*key) for key in others], rows_dev)):
                soon["p", *key] = part
            ours, theirs = pick(acts, cotan, block_ids, core)
            scales = (1.0 / samples, tokens / samples)
            soon["keep"], away = terms(flags[1:], ours, swap_core(theirs), block_size, scales)
            late["back"] = swap_x(away)
            for j, at, _ in [key for key in first + others if key[2] == 1]:
                when = soon if (j, at) == (0, 0) else late
                got = {**env, **soon}
                when["c", 0, j, at, 0] = got["p", j, at, 0]
                when["c", 0, j, at, 1] = swap_core(got["p", j, at, 1])
        for item, when in y_stage.items():
            if when == stage:
                step, j, at, flip = item
                late["c", step, j, at, flip] = from_worker(env["p", j, at, flip], step, flip)
        for step, j, n in x_items:
            if x_stage[step, j, n] == stage:
                late["got", step, j, n] = swap_x(env.pop(("out", step, j, n)))
        for (step, j, n, at), when in z_stage.items():
            if when == stage:
                late["hop", step, j, n] = hop(env["acc", step, j, n], hops_of(step, j)[at])

        ready = {**env, **soon} if stage == 0 else env
        due = [key for key, when in product_stage.items() if when == stage]
        if due:
            pairs = [[ready["c", step, j, at, flip] for flip in range(2)] for step, j, at in due]
            found = products(pairs, (ready["acts"], ready["acts_sib"]), len(starts))
            for (step, j, at), outs in zip(due, found):
                for n, out in enumerate(outs):
                    soon["mine" if at else "out", step, j, n] = out

        if stage == 2:
            half = (env.pop("keep") + env.pop("back")).reshape(n_z, -1, block_size)
            soon["quarter"] = lax.dynamic_index_in_dim(half, z, 0, keepdims=False)
            for far in range(1, n_z):
                away = lax.dynamic_index_in_dim(half, (z + far) % n_z, 0, keepdims=False)
                late["quarter", far] = swap_z(away, far)
        if stage == 4:
            total = env.pop("quarter").astype(F32)
            for far in range(1, n_z):
                total = total + env.pop(("quarter", far)).astype(F32)
            soon["whole", 0] = total.astype(BF16)
        if stage == 5:
            for far in range(1, n_z):
                late["whole", far] = swap_z(env["whole", 0], far)
        if stage == 7:
            half = jnp.zeros((n_z, *env["whole", 0].shape), BF16)
            for far in range(n_z):
                half = lax.dynamic_update_index_in_dim(half, env.pop(("whole", far)), (z - far) % n_z, 0)
            soon["keep"] = half.reshape(local_blocks, -1, block_size)
        if stage == 8:
            late["back"] = swap_x(env["keep"])
            late["keep_sib"] = swap_core(env["keep"])
        if stage == 10:
            late["back_sib"] = swap_core(env["back"])
        if stage == max(12, last - 1):
            act_new, grad_new, eig_in, eig_local = update_factors(
                flags,
                [env.pop(key) for key in ("keep", "back", "keep_sib", "back_sib")],
                (act_factor, grad_factor),
                basis_in,
                basis_out,
            )

        env.update(soon)
        env.update(pending)
        pending = late
        for step, j, n in x_items:
            mine, got, acc = ("mine", step, j, n), ("got", step, j, n), ("acc", step, j, n)
            if mine in env and got in env:
                env[acc] = env.pop(mine) + env.pop(got)
            if ("hop", step, j, n) in env:
                env[acc] = env[acc] + env.pop(("hop", step, j, n))
        for n in range(len(starts)):
            final = [z_stage[step, j, n, len(hops_of(step, j)) - 1] for step, j in shards]
            if stage == max(final) + DEPTH - 1:
                total = None
                for step, j in shards:
                    ends = jnp.array([place((i + step) % n_worker, j) for i in range(n_worker)], jnp.int32)
                    acc = env.pop(("acc", step, j, n))
                    total = acc if total is None else jnp.where(ends[w] == z, acc, total)
                done[n] = total

    eig_block = jnp.zeros((block_size,), F32)
    for step in range(n_worker):
        held = eig_local if step == 0 else from_worker(eig_local, step, 0)
        row = lax.dynamic_index_in_dim(held, block % local_blocks, 0, keepdims=False)[0]
        owner = (w + step) % n_worker
        eig_block = jnp.where(owner == block // local_blocks, row, eig_block)

    sharers = block_size // rows_dev
    spot = jnp.stack([block, d % sharers]).astype(jnp.int32)
    precond = None
    for n in range(len(starts)):
        parts = [done[n]]
        for step in range(1, sharers):
            pairs = [(i, i // sharers * sharers + (i + step) % sharers) for i in range(n_dp)]
            parts.append(lax.ppermute(parts[0], "dp", pairs))
        precond = tail(spot, parts, basis_in, basis_out, eig_in, eig_block[:, None], n, precond)
    return precond, act_new, grad_new


def solution(mesh):
    return jax.shard_map(
        per_device,
        mesh=mesh,
        in_specs=(
            P("dp", "worker"),
            P("dp", "worker"),
            P("dp"),
            P("worker", None, None),
            P(),
            P("worker", None, None),
            P("worker", None, None),
        ),
        out_specs=(P("dp", "worker"), P("worker", None, None), P("worker", None, None)),
        check_vma=False,
    )
```

```python
import functools

import jax
import jax.numpy as jnp
from jax import lax
from jax.experimental import pallas as pl
from jax.experimental.pallas import tpu as pltpu
from jax.sharding import PartitionSpec as P

BLK = 128
QUARTER = 128
VMEM = 56 * 2**20
SLOTS = 5
COL_CHUNKS = 2


DECAY_RATE = 0.75
DAMPING = 0.03

BF16 = jnp.bfloat16
F32 = jnp.float32

SMALL = pl.CostEstimate(flops=1, bytes_accessed=1, transcendentals=0)


def pick_kernel(n_picks, which_ref, acts, cotan, ours, theirs):
    is_act = which_ref[n_picks] == 0
    ours[...] = jnp.where(is_act, acts[...], cotan[...])
    theirs[...] = jnp.where(is_act, cotan[...], acts[...])


def pick(acts, cotan, block_ids, core):
    n_picks, width = block_ids.shape[0], acts.shape[1]
    chosen = pl.BlockSpec((BLK, width), lambda i, which: (which[i], 0))
    out = pl.BlockSpec((BLK, width), lambda i, which: (i, 0))
    return pl.pallas_call(
        functools.partial(pick_kernel, n_picks),
        grid_spec=pltpu.PrefetchScalarGridSpec(
            num_scalar_prefetch=1, grid=(n_picks,), in_specs=[chosen] * 2, out_specs=[out] * 2
        ),
        out_shape=[jax.ShapeDtypeStruct((n_picks * BLK, width), BF16)] * 2,
        compiler_params=pltpu.CompilerParams(vmem_limit_bytes=VMEM),
        cost_estimate=SMALL,
    )(jnp.concatenate([block_ids, jnp.reshape(core, (1,))]).astype(jnp.int32), acts, cotan)


def pack_upper(full):
    q = QUARTER
    second = jnp.concatenate([full[q : 2 * q, q:], full[3 * q :, 3 * q :]], axis=1)
    third = full[2 * q : 3 * q, 2 * q :]
    third = jnp.concatenate([third[: q // 2], third[q // 2 :]], axis=1)
    return jnp.concatenate([full[:q], second, third], axis=0)


def term_kernel(scales, place_ref, ours, theirs, keep, away):
    total = 0.0
    for rows in (ours[...], theirs[...]):
        total = total + lax.dot_general(
            rows, rows, (((0,), (0,)), ((), ())), preferred_element_type=F32
        )
    scale = jnp.where(place_ref[0] == 0, scales[0], scales[1]).astype(F32)
    packed = pack_upper(total * scale)
    half = packed.shape[0] // 2
    low = place_ref[1] == 0
    keep[0] = jnp.where(low, packed[:half], packed[half:]).astype(BF16)
    away[0] = jnp.where(low, packed[half:], packed[:half]).astype(BF16)


def terms(place, ours, theirs, size, scales):
    rows, width = ours.shape
    blocks, half = width // size, 5 * QUARTER // 4
    strip = pl.BlockSpec((rows, size), lambda b, place: (0, b))
    out = pl.BlockSpec((1, half, size), lambda b, place: (b, 0, 0))
    return pl.pallas_call(
        functools.partial(term_kernel, scales),
        grid_spec=pltpu.PrefetchScalarGridSpec(
            num_scalar_prefetch=1, grid=(blocks,), in_specs=[strip] * 2, out_specs=[out] * 2
        ),
        out_shape=[jax.ShapeDtypeStruct((blocks, half, size), BF16)] * 2,
        compiler_params=pltpu.CompilerParams(vmem_limit_bytes=VMEM),
        cost_estimate=SMALL,
    )(place, ours, theirs)


def unpack_upper(packed):
    q = QUARTER
    tiles = {}
    for j in range(4):
        tiles[0, j] = packed[:q, j * q : (j + 1) * q]
    for j in range(1, 4):
        tiles[1, j] = packed[q : 2 * q, (j - 1) * q : j * q]
    tiles[3, 3] = packed[q : 2 * q, 3 * q :]
    third = jnp.concatenate([packed[2 * q :, : 2 * q], packed[2 * q :, 2 * q :]], axis=0)
    tiles[2, 2], tiles[2, 3] = third[:, :q], third[:, q:]
    return [[tiles[i, j] if j >= i else tiles[j, i].T for j in range(4)] for i in range(4)]


def factor_kernel(place_ref, low, high, low_sib, high_sib, *refs):
    for kind, (factor, basis, new, eig) in enumerate(zip(refs[0:2], refs[2:4], refs[4:6], refs[6:8])):
        here = place_ref[1] == kind
        halves = [jnp.where(here, low[0], low_sib[0]), jnp.where(here, high[0], high_sib[0])]
        rows = unpack_upper(jnp.concatenate(halves, axis=0).astype(F32))
        q = QUARTER
        for i in range(4):
            for j in range(4):
                at = (0, pl.ds(i * q, q), pl.ds(j * q, q))
                new[at] = DECAY_RATE * factor[at] + (1.0 - DECAY_RATE) * rows[i][j]
        vectors = basis[0]
        rest = new[0]
        product = 0.0
        for _ in range(3):
            part = rest.astype(BF16)
            rest = rest - part.astype(F32)
            product = product + jnp.dot(part, vectors, preferred_element_type=F32)
        eig[0] = jnp.sum(vectors.astype(F32) * product, axis=0, keepdims=True)


def update_factors(place, halves, factors, basis_in, basis_out):
    blocks, size, _ = basis_in.shape

    def local(b, place):
        return (b, 0, 0)

    square = pl.BlockSpec((1, size, size), local)
    narrow = pl.BlockSpec((1, halves[0].shape[1], size), local)
    line = pl.BlockSpec((1, 1, size), local)
    return pl.pallas_call(
        factor_kernel,
        grid_spec=pltpu.PrefetchScalarGridSpec(
            num_scalar_prefetch=1,
            grid=(blocks,),
            in_specs=[narrow] * 4
            + [square] * 3
            + [pl.BlockSpec((1, size, size), lambda b, place: (place[0] + b, 0, 0))],
            out_specs=[square, square, line, line],
        ),
        out_shape=[jax.ShapeDtypeStruct((blocks, size, size), F32)] * 2
        + [jax.ShapeDtypeStruct((blocks, 1, size), F32)] * 2,
        compiler_params=pltpu.CompilerParams(vmem_limit_bytes=VMEM),
        cost_estimate=SMALL,
    )(place, *halves, *factors, basis_in, basis_out)


def tail_kernel(n_parts, place_ref, *refs):
    parts, (basis, outer, eig_in, eig_out) = refs[:n_parts], refs[n_parts : n_parts + 4]
    out, whole = refs[-2:]
    sharers = len(parts)
    rows = parts[0].shape[0]
    me = place_ref[1]
    for step, part in enumerate(parts):
        spot = lax.rem(me - step + sharers, sharers)
        whole[pl.ds(pl.multiple_of(spot * rows, rows), rows), :] = part[...]
    right = jnp.dot(whole[...], basis[0], preferred_element_type=F32).astype(BF16)
    inner = lax.dot_general(outer[0], right, (((0,), (0,)), ((), ())), preferred_element_type=F32)
    column = jnp.broadcast_to(eig_out[0], (QUARTER, eig_out.shape[2])).T[:, :1]
    scaled = (inner / (column * eig_in[0] + DAMPING)).astype(BF16)
    mine = outer[0, pl.ds(pl.multiple_of(me * rows, rows), rows), :]
    upper = jnp.dot(mine, scaled, preferred_element_type=F32).astype(BF16)
    out[...] = lax.dot_general(
        upper, basis[0], (((1,), (1,)), ((), ())), preferred_element_type=F32
    ).astype(BF16)


def tail(place, parts, basis_in, basis_out, eig_in, eig_out, chunk, filled):
    blocks, size, _ = basis_in.shape
    rows, cols = parts[0].shape
    each = cols // size
    strip = pl.BlockSpec((rows, size), lambda b, place: (0, b))
    in_specs = [strip] * len(parts) + [
        pl.BlockSpec((1, size, size), lambda b, place: (chunk * each + b, 0, 0)),
        pl.BlockSpec((1, size, size), lambda b, place: (place[0], 0, 0)),
        pl.BlockSpec((1, 1, size), lambda b, place: (chunk * each + b, 0, 0)),
        pl.BlockSpec((1, 1, size), lambda b, place: (place[2], 0, 0)),
    ]
    args = [place, *parts, basis_in, basis_out, eig_in, eig_out]
    aliases = {}
    if filled is not None:
        in_specs.append(pl.BlockSpec(memory_space=pl.ANY))
        aliases = {len(args): 0}
        args.append(filled)
    return pl.pallas_call(
        functools.partial(tail_kernel, len(parts)),
        grid_spec=pltpu.PrefetchScalarGridSpec(
            num_scalar_prefetch=1,
            grid=(each,),
            in_specs=in_specs,
            out_specs=pl.BlockSpec((rows, size), lambda b, place: (0, chunk * each + b)),
            scratch_shapes=[pltpu.VMEM((size, size), BF16)],
        ),
        out_shape=jax.ShapeDtypeStruct((rows, blocks * size), BF16),
        input_output_aliases=aliases,
        compiler_params=pltpu.CompilerParams(vmem_limit_bytes=VMEM),
        cost_estimate=pl.CostEstimate(
            flops=each * 6 * size**3, bytes_accessed=4 * each * size**2, transcendentals=0
        ),
    )(*args)


def turn_kernel(which_ref, block, *outs):
    del which_ref
    step = pl.program_id(0)
    for n, out in enumerate(outs):

        @pl.when((step == n) | ((n == 4) & (step >= 2)))
        def _(out=out):
            out[...] = block[...].T


def turned(rows, which, n_rows):
    tokens, _ = rows.shape
    one = pl.BlockSpec((n_rows, tokens), lambda i, which: (0, 0))
    return pl.pallas_call(
        turn_kernel,
        grid_spec=pltpu.PrefetchScalarGridSpec(
            num_scalar_prefetch=1,
            grid=(4,),
            in_specs=[pl.BlockSpec((tokens, n_rows), lambda i, which: (0, which[i]))],
            out_specs=[one] * 4
            + [pl.BlockSpec((n_rows, tokens), lambda i, which: (jnp.clip(i - 2, 0, 1), 0))],
        ),
        out_shape=[jax.ShapeDtypeStruct((n_rows, tokens), BF16)] * 4
        + [jax.ShapeDtypeStruct((2 * n_rows, tokens), BF16)],
        compiler_params=pltpu.CompilerParams(vmem_limit_bytes=VMEM),
        cost_estimate=SMALL,
    )(jnp.stack(which).astype(jnp.int32), rows)


def product_kernel(counts, n_outs, *refs):
    n_left = sum(counts)
    halves = refs[: counts[0]], refs[counts[0] : n_left]
    right, outs, left = refs[n_left : n_left + 2], refs[n_left + 2 : -1], refs[-1]
    step = pl.program_id(0)
    tokens = right[0].shape[0]

    @pl.when(step == 0)
    def _():
        for half, pieces in enumerate(halves):
            row = 0
            for piece in pieces:
                left[row : row + piece.shape[0], half * tokens : (half + 1) * tokens] = piece[...]
                row += piece.shape[0]

    total = jnp.dot(left[:, :tokens], right[0][...], preferred_element_type=F32)
    total = total + jnp.dot(left[:, tokens:], right[1][...], preferred_element_type=F32)
    chunks = len(outs) // n_outs
    rows = left.shape[0] // n_outs
    each = pl.num_programs(0) // chunks
    for n in range(chunks):

        @pl.when(step // each == n)
        def _(n=n):
            for at in range(n_outs):
                outs[at * chunks + n][...] = total[at * rows : (at + 1) * rows].astype(BF16)


def products(halves, n_outs, rows, chunks):
    tokens, width = rows[0].shape
    n_rows = sum(piece.shape[0] for piece in halves[0])
    tile = 512
    each = width // chunks // tile
    strip = pl.BlockSpec((tokens, tile), lambda i: (0, i))
    outs = pl.pallas_call(
        functools.partial(product_kernel, [len(half) for half in halves], n_outs),
        grid=(width // tile,),
        in_specs=[pl.BlockSpec(p.shape, lambda i: (0, 0)) for half in halves for p in half] + [strip] * 2,
        out_specs=[
            pl.BlockSpec((n_rows // n_outs, tile), lambda i, n=n: (0, jnp.clip(i - n * each, 0, each - 1)))
            for _ in range(n_outs)
            for n in range(chunks)
        ],
        out_shape=[jax.ShapeDtypeStruct((n_rows // n_outs, width // chunks), BF16)] * (n_outs * chunks),
        scratch_shapes=[pltpu.VMEM((n_rows, 2 * tokens), BF16)],
        compiler_params=pltpu.CompilerParams(vmem_limit_bytes=VMEM),
        cost_estimate=SMALL,
    )(*halves[0], *halves[1], *rows)
    return [outs[m * chunks : (m + 1) * chunks] for m in range(n_outs)]


def per_device(acts, cotan, block_ids, basis_in, basis_out, act_factor, grad_factor):
    n_dp = lax.axis_size("dp")
    n_worker = lax.axis_size("worker")
    d = lax.axis_index("dp")
    w = lax.axis_index("worker")
    core, x = d % 2, (d // 2) % 2
    n_z = n_dp // 4
    pool_rows, width = acts.shape
    local_blocks, block_size, _ = basis_in.shape
    model_width = basis_out.shape[0] * block_size
    samples = block_ids.shape[0] * BLK * n_dp
    tokens = pool_rows * n_dp
    rows_dev = model_width // n_dp
    z_per_worker = n_z // n_worker
    cols = width // COL_CHUNKS if width >= 1024 else width
    both = ("dp", "worker")

    def swap_core(v):
        return lax.ppermute(v, "dp", [(i, i ^ 1) for i in range(n_dp)])

    def swap_x(v):
        return lax.ppermute(v, "dp", [(i, i ^ 2) for i in range(n_dp)])

    def from_worker(v, step, flip):
        return lax.ppermute(
            v,
            both,
            [
                ((i ^ flip) * n_worker + (j + step) % n_worker, i * n_worker + j)
                for i in range(n_dp)
                for j in range(n_worker)
            ],
        )

    def place(owner, j):
        return owner * z_per_worker + (j if owner < n_worker // 2 else z_per_worker - 1 - j)

    z = d // 4
    starts = list(range(0, width, cols))
    shards = [(0, j) for j in range(z_per_worker)]
    shards += [(step, j) for j in range(z_per_worker) for step in range(1, n_worker)]

    def hops_of(step, j):
        hops = []
        size = 1
        while size < n_z:
            moves = []
            for i in range(n_worker):
                end = place((i + step) % n_worker, j)
                for low in range(0, n_z, 2 * size):
                    heads = [min(max(end, at), at + size - 1) for at in (low, low + size)]
                    to = min(max(end, low), low + 2 * size - 1)
                    moves.append((i, sum(heads) - to, to))
            hops.append(moves)
            size *= 2
        return hops

    def links(moves):
        found = set()
        for i, a, b in moves:
            ahead = 1 if b > a else -1
            found.update((i, at, at + ahead) for at in range(a, b, ahead))
        return found

    def swap_z(v, bit):
        return lax.ppermute(v, "dp", [(i, i ^ (4 * bit)) for i in range(n_dp)])

    def hop(v, moves):
        pairs = [((a * 4 + r) * n_worker + i, (b * 4 + r) * n_worker + i) for i, a, b in moves for r in range(4)]
        return lax.ppermute(v, both, pairs)

    def piece(j, at, flip):
        part = jnp.where(w < n_worker // 2, j, z_per_worker - 1 - j)
        x_to = x if at else 1 - x
        core_to = 1 - core if flip else core
        return (part * 2 + x_to) * 2 + core_to

    chunks = range(len(starts))
    used = {}

    def hold(stage):
        used[stage] = used.get(stage, 0) + 1

    x_stage, z_stage, busy = {}, {}, set()
    y_items = [(step, j, at, flip) for step, j in shards if step for at in range(2) for flip in range(2)]
    y_stage = {item: max(0, at - 1) for at, item in enumerate(y_items)}
    for stage in y_stage.values():
        hold(stage)
    product_stage = {(0, 0, 0): 0, (0, 0, 1): 0}
    clock = 0
    for step, j in shards:
        if step == 0 and j:
            product_stage[0, j, 0] = product_stage[0, j, 1] = clock
        if step:
            here, there = y_stage[step, j, 0, 1] + 1, y_stage[step, j, 1, 1] + 1
            product_stage[step, j, 0] = there if there <= clock else max(here, clock - 1)
            product_stage[step, j, 1] = there
            clock = max(clock, product_stage[step, j, 0])
        for n in chunks:
            clock += 1
            x_stage[step, j, n] = clock
            hold(clock)
    z_bits = [2**bit for bit in range((n_z - 1).bit_length())]
    hold(1)
    scatter = [1 + at for at in range(len(z_bits))]
    across = scatter[-1] + 1
    gather = [across + 1 + at for at in range(len(z_bits))]
    between = gather[-1] + 1
    for stage in range(1, between + 1):
        hold(stage)
    fresh = between + 1
    while fresh in product_stage.values():
        fresh += 1
    hold(fresh + 1)
    for n_hop in range(len(z_bits)):
        for step, j, n in x_stage:
            ready = max(x_stage[step, j, n], product_stage[step, j, 1])
            clock = (z_stage[step, j, n, n_hop - 1] if n_hop else ready) + 1
            moves = links(hops_of(step, j)[n_hop])
            while used.get(clock, 0) >= SLOTS or any((clock, link) in busy for link in moves):
                clock += 1
            busy.update((clock, link) for link in moves)
            z_stage[step, j, n, n_hop] = clock
            hold(clock)
    last = max(*z_stage.values(), fresh + 1)

    my_start = d * rows_dev
    block = my_start // block_size
    flags = jnp.stack([w * local_blocks, core, x]).astype(jnp.int32)
    env = {"acts": acts, "cotan": cotan}
    done = {}

    def turn(rows, j):
        which = [piece(j, at, flip) for flip in range(2) for at in range(2)]
        *single, both_rows = turned(rows, which, rows_dev)
        found = {("p", j, at, flip): single[2 * flip + at] for flip in range(2) for at in range(2)}
        return {**found, ("p", j): both_rows}

    def in_order(bit, mine, theirs):
        return jnp.where(bit == 0, jnp.stack([mine, theirs]), jnp.stack([theirs, mine]))

    for stage in range(last + 1):
        if stage:
            keys = sorted(env, key=str)
            env = dict(zip(keys, lax.optimization_barrier(tuple(env[k] for k in keys))))
        joined = {}
        if stage == 0:
            joined["acts_sib"] = swap_core(acts)
            env.update(turn(cotan, 0))
            ours, theirs = pick(acts, cotan, block_ids, core)
            scales = (1.0 / samples, tokens / samples)
            keep, away = terms(flags[1:], ours, swap_core(theirs), block_size, scales)
            away = swap_x(away)
            joined["c", 0] = swap_core(env.pop(("p", 0)))
        if stage == 1:
            for j in range(1, z_per_worker):
                found = turn(env["cotan"], j)
                joined["c", j] = swap_core(found.pop(("p", j)))
                joined.update(found)
        for (step, j, at, flip), when in y_stage.items():
            if when == stage:
                joined["c", step, j, at, flip] = from_worker(env["p", j, at, flip], step, flip)
        for (step, j, n), when in x_stage.items():
            if when == stage:
                joined["got", step, j, n] = swap_x(env.pop(("out", step, j, n)))
        for (step, j, n, at), when in z_stage.items():
            if when == stage:
                joined["hop", step, j, n] = hop(env["acc", step, j, n], hops_of(step, j)[at])

        for at, when in enumerate(scatter):
            if stage == when:
                bit = z // z_bits[at] % 2
                parts = env["keep"].reshape(2, -1, block_size)
                there = lax.dynamic_index_in_dim(parts, 1 - bit, 0, keepdims=False)
                here = lax.dynamic_index_in_dim(parts, bit, 0, keepdims=False)
                joined["keep"] = here + swap_z(there, z_bits[at])
        if stage == across:
            joined["keep"] = in_order(x, env["keep"], swap_x(env["keep"]))[None]
        for at, when in enumerate(gather):
            if stage == when:
                far = z_bits[-1 - at]
                joined["keep"] = in_order(z // far % 2, env["keep"], swap_z(env["keep"], far))
                joined["keep"] = joined["keep"].reshape(-1, *env["keep"].shape[1:])
        if stage == between:
            full = jnp.swapaxes(env["keep"], 0, 1).reshape(2, local_blocks, -1, block_size)
            joined["low"], joined["high"] = full[0], full[1]
            joined["other"] = swap_core(env["keep"])
            joined.pop("keep", None)
        if stage == fresh:
            full = jnp.swapaxes(env.pop("other"), 0, 1).reshape(2, local_blocks, -1, block_size)
            act_new, grad_new, joined["eig_in"], eig_local = update_factors(
                flags,
                [env.pop("low"), env.pop("high"), full[0], full[1]],
                (act_factor, grad_factor),
                basis_in,
                basis_out,
            )
            joined["eigs"] = eig_local
            done["factors"] = act_new, grad_new
        if stage == fresh + 1:
            eigs = [env["eigs"]] + [from_worker(env["eigs"], step, 0) for step in range(1, n_worker)]
            joined["eigs"] = jnp.concatenate(eigs, axis=0)

        for step, j in shards:
            due = [at for at in range(2) if product_stage[step, j, at] == stage]
            if due:
                known = {**env, **joined} if stage == 0 else env
                if step == 0:
                    halves = [[known["p", j, at, 0] for at in range(2)], [known["c", j]]]
                else:
                    halves = [[known["c", step, j, at, flip] for at in due] for flip in range(2)]
                found = products(halves, len(due), (known["acts"], known["acts_sib"]), len(starts))
                for at, outs in zip(due, found):
                    for n in chunks:
                        joined["mine" if at else "out", step, j, n] = outs[n]
        if stage == 0:
            keep, joined["out", 0, 0, 0] = lax.optimization_barrier((keep, joined["out", 0, 0, 0]))
            joined["keep"] = keep + away
        env.update(joined)
        for step, j, n in x_stage:
            mine, got, acc = ("mine", step, j, n), ("got", step, j, n), ("acc", step, j, n)
            if mine in env and got in env:
                env[acc] = env.pop(mine) + env.pop(got)
            if ("hop", step, j, n) in env:
                env[acc] = env[acc] + env.pop(("hop", step, j, n))
        for n in chunks:
            if stage == max(z_stage[step, j, n, len(z_bits) - 1] for step, j in shards):
                total = None
                for step, j in shards:
                    ends = jnp.array([place((i + step) % n_worker, j) for i in range(n_worker)], jnp.int32)
                    acc = env.pop(("acc", step, j, n))
                    total = acc if total is None else jnp.where(ends[w] == z, acc, total)
                done[n] = total

    act_new, grad_new = done["factors"]
    eig_in, eig_out = env["eig_in"], env["eigs"]
    held = (block // local_blocks - w) % n_worker * local_blocks + block % local_blocks

    sharers = block_size // rows_dev
    spot = jnp.stack([block, d % sharers, held]).astype(jnp.int32)
    precond = None
    for n in range(len(starts)):
        parts = [done[n]]
        for step in range(1, sharers):
            pairs = [(i, i // sharers * sharers + (i + step) % sharers) for i in range(n_dp)]
            parts.append(lax.ppermute(parts[0], "dp", pairs))
        precond = tail(spot, parts, basis_in, basis_out, eig_in, eig_out, n, precond)
    return precond, act_new, grad_new


def solution(mesh):
    return jax.shard_map(
        per_device,
        mesh=mesh,
        in_specs=(
            P("dp", "worker"),
            P("dp", "worker"),
            P("dp"),
            P("worker", None, None),
            P(),
            P("worker", None, None),
            P("worker", None, None),
        ),
        out_specs=(P("dp", "worker"), P("worker", None, None), P("worker", None, None)),
        check_vma=False,
    )
```

```python
import functools

import jax
import jax.numpy as jnp
from jax import lax
from jax.experimental import pallas as pl
from jax.experimental.pallas import tpu as pltpu
from jax.sharding import PartitionSpec as P

BLK = 128
QUARTER = 128
VMEM = 56 * 2**20
COL_CHUNKS = 1


DECAY_RATE = 0.75
DAMPING = 0.03

BF16 = jnp.bfloat16
F32 = jnp.float32

SMALL = pl.CostEstimate(flops=1, bytes_accessed=1, transcendentals=0)


def pick_kernel(n_picks, which_ref, acts, cotan, ours, theirs):
    is_act = which_ref[n_picks] == 0
    ours[...] = jnp.where(is_act, acts[...], cotan[...])
    theirs[...] = jnp.where(is_act, cotan[...], acts[...])


def pick(acts, cotan, block_ids, core):
    n_picks, width = block_ids.shape[0], acts.shape[1]
    chosen = pl.BlockSpec((BLK, width), lambda i, which: (which[i], 0))
    out = pl.BlockSpec((BLK, width), lambda i, which: (i, 0))
    return pl.pallas_call(
        functools.partial(pick_kernel, n_picks),
        grid_spec=pltpu.PrefetchScalarGridSpec(
            num_scalar_prefetch=1, grid=(n_picks,), in_specs=[chosen] * 2, out_specs=[out] * 2
        ),
        out_shape=[jax.ShapeDtypeStruct((n_picks * BLK, width), BF16)] * 2,
        compiler_params=pltpu.CompilerParams(vmem_limit_bytes=VMEM),
        cost_estimate=SMALL,
    )(jnp.concatenate([block_ids, jnp.reshape(core, (1,))]).astype(jnp.int32), acts, cotan)


def pack_upper(full):
    q = QUARTER
    second = jnp.concatenate([full[q : 2 * q, q:], full[3 * q :, 3 * q :]], axis=1)
    third = full[2 * q : 3 * q, 2 * q :]
    third = jnp.concatenate([third[: q // 2], third[q // 2 :]], axis=1)
    return jnp.concatenate([full[:q], second, third], axis=0)


def term_kernel(scales, place_ref, ours, theirs, keep, away):
    total = 0.0
    for rows in (ours[...], theirs[...]):
        total = total + lax.dot_general(
            rows, rows, (((0,), (0,)), ((), ())), preferred_element_type=F32
        )
    scale = jnp.where(place_ref[0] == 0, scales[0], scales[1]).astype(F32)
    packed = pack_upper(total * scale)
    half = packed.shape[0] // 2
    low = place_ref[1] == 0
    keep[0] = jnp.where(low, packed[:half], packed[half:]).astype(BF16)
    away[0] = jnp.where(low, packed[half:], packed[:half]).astype(BF16)


def terms(place, ours, theirs, size, scales):
    rows, width = ours.shape
    blocks, half = width // size, 5 * QUARTER // 4
    strip = pl.BlockSpec((rows, size), lambda b, place: (0, b))
    out = pl.BlockSpec((1, half, size), lambda b, place: (b, 0, 0))
    return pl.pallas_call(
        functools.partial(term_kernel, scales),
        grid_spec=pltpu.PrefetchScalarGridSpec(
            num_scalar_prefetch=1, grid=(blocks,), in_specs=[strip] * 2, out_specs=[out] * 2
        ),
        out_shape=[jax.ShapeDtypeStruct((blocks, half, size), BF16)] * 2,
        compiler_params=pltpu.CompilerParams(vmem_limit_bytes=VMEM),
        cost_estimate=SMALL,
    )(place, ours, theirs)


def unpack_upper(packed):
    q = QUARTER
    tiles = {}
    for j in range(4):
        tiles[0, j] = packed[:q, j * q : (j + 1) * q]
    for j in range(1, 4):
        tiles[1, j] = packed[q : 2 * q, (j - 1) * q : j * q]
    tiles[3, 3] = packed[q : 2 * q, 3 * q :]
    third = jnp.concatenate([packed[2 * q :, : 2 * q], packed[2 * q :, 2 * q :]], axis=0)
    tiles[2, 2], tiles[2, 3] = third[:, :q], third[:, q:]
    return [[tiles[i, j] if j >= i else tiles[j, i].T for j in range(4)] for i in range(4)]


def factor_kernel(place_ref, keep, back, keep_sib, back_sib, *refs):
    low = place_ref[2] == 0
    for kind, (factor, basis, new, eig) in enumerate(zip(refs[0:2], refs[2:4], refs[4:6], refs[6:8])):
        here = place_ref[1] == kind
        kept = jnp.where(here, keep[0], keep_sib[0])
        came = jnp.where(here, back[0], back_sib[0])
        halves = [jnp.where(low, kept, came), jnp.where(low, came, kept)]
        rows = unpack_upper(jnp.concatenate(halves, axis=0).astype(F32))
        q = QUARTER
        for i in range(4):
            for j in range(4):
                at = (0, pl.ds(i * q, q), pl.ds(j * q, q))
                new[at] = DECAY_RATE * factor[at] + (1.0 - DECAY_RATE) * rows[i][j]
        vectors = basis[0]
        rest = new[0]
        product = 0.0
        for _ in range(3):
            part = rest.astype(BF16)
            rest = rest - part.astype(F32)
            product = product + jnp.dot(part, vectors, preferred_element_type=F32)
        eig[0] = jnp.sum(vectors.astype(F32) * product, axis=0, keepdims=True)


def update_factors(place, halves, factors, basis_in, basis_out):
    blocks, size, _ = basis_in.shape

    def local(b, place):
        return (b, 0, 0)

    square = pl.BlockSpec((1, size, size), local)
    narrow = pl.BlockSpec((1, halves[0].shape[1], size), local)
    line = pl.BlockSpec((1, 1, size), local)
    return pl.pallas_call(
        factor_kernel,
        grid_spec=pltpu.PrefetchScalarGridSpec(
            num_scalar_prefetch=1,
            grid=(blocks,),
            in_specs=[narrow] * 4
            + [square] * 3
            + [pl.BlockSpec((1, size, size), lambda b, place: (place[0] + b, 0, 0))],
            out_specs=[square, square, line, line],
        ),
        out_shape=[jax.ShapeDtypeStruct((blocks, size, size), F32)] * 2
        + [jax.ShapeDtypeStruct((blocks, 1, size), F32)] * 2,
        compiler_params=pltpu.CompilerParams(vmem_limit_bytes=VMEM),
        cost_estimate=SMALL,
    )(place, *halves, *factors, basis_in, basis_out)


def tail_kernel(n_parts, place_ref, *refs):
    parts, (basis, outer, eig_in, eig_out) = refs[:n_parts], refs[n_parts : n_parts + 4]
    out, whole = refs[-2:]
    sharers = len(parts)
    rows = parts[0].shape[0]
    me = place_ref[1]
    for step, part in enumerate(parts):
        spot = lax.rem(me - step + sharers, sharers)
        whole[pl.ds(pl.multiple_of(spot * rows, rows), rows), :] = part[...]
    right = jnp.dot(whole[...], basis[0], preferred_element_type=F32).astype(BF16)
    inner = lax.dot_general(outer[0], right, (((0,), (0,)), ((), ())), preferred_element_type=F32)
    column = jnp.broadcast_to(eig_out[0], (QUARTER, eig_out.shape[2])).T[:, :1]
    scaled = (inner / (column * eig_in[0] + DAMPING)).astype(BF16)
    mine = outer[0, pl.ds(pl.multiple_of(me * rows, rows), rows), :]
    upper = jnp.dot(mine, scaled, preferred_element_type=F32).astype(BF16)
    out[...] = lax.dot_general(
        upper, basis[0], (((1,), (1,)), ((), ())), preferred_element_type=F32
    ).astype(BF16)


def tail(place, parts, basis_in, basis_out, eig_in, eig_out, chunk, filled):
    blocks, size, _ = basis_in.shape
    rows, cols = parts[0].shape
    each = cols // size
    strip = pl.BlockSpec((rows, size), lambda b, place: (0, b))
    in_specs = [strip] * len(parts) + [
        pl.BlockSpec((1, size, size), lambda b, place: (chunk * each + b, 0, 0)),
        pl.BlockSpec((1, size, size), lambda b, place: (place[0], 0, 0)),
        pl.BlockSpec((1, 1, size), lambda b, place: (chunk * each + b, 0, 0)),
        pl.BlockSpec((1, 1, size), lambda b, place: (place[2], 0, 0)),
    ]
    args = [place, *parts, basis_in, basis_out, eig_in, eig_out]
    aliases = {}
    if filled is not None:
        in_specs.append(pl.BlockSpec(memory_space=pl.ANY))
        aliases = {len(args): 0}
        args.append(filled)
    return pl.pallas_call(
        functools.partial(tail_kernel, len(parts)),
        grid_spec=pltpu.PrefetchScalarGridSpec(
            num_scalar_prefetch=1,
            grid=(each,),
            in_specs=in_specs,
            out_specs=pl.BlockSpec((rows, size), lambda b, place: (0, chunk * each + b)),
            scratch_shapes=[pltpu.VMEM((size, size), BF16)],
        ),
        out_shape=jax.ShapeDtypeStruct((rows, blocks * size), BF16),
        input_output_aliases=aliases,
        compiler_params=pltpu.CompilerParams(vmem_limit_bytes=VMEM),
        cost_estimate=pl.CostEstimate(
            flops=each * 6 * size**3, bytes_accessed=4 * each * size**2, transcendentals=0
        ),
    )(*args)


def turn_kernel(which_ref, block, *outs):
    del which_ref
    step = pl.program_id(0)
    for n, out in enumerate(outs):

        @pl.when((step == n) | ((n == 4) & (step >= 2)))
        def _(out=out):
            out[...] = block[...].T


def turned(rows, which, n_rows):
    tokens, _ = rows.shape
    one = pl.BlockSpec((n_rows, tokens), lambda i, which: (0, 0))
    return pl.pallas_call(
        turn_kernel,
        grid_spec=pltpu.PrefetchScalarGridSpec(
            num_scalar_prefetch=1,
            grid=(4,),
            in_specs=[pl.BlockSpec((tokens, n_rows), lambda i, which: (0, which[i]))],
            out_specs=[one] * 4
            + [pl.BlockSpec((n_rows, tokens), lambda i, which: (jnp.clip(i - 2, 0, 1), 0))],
        ),
        out_shape=[jax.ShapeDtypeStruct((n_rows, tokens), BF16)] * 4
        + [jax.ShapeDtypeStruct((2 * n_rows, tokens), BF16)],
        compiler_params=pltpu.CompilerParams(vmem_limit_bytes=VMEM),
        cost_estimate=SMALL,
    )(jnp.stack(which).astype(jnp.int32), rows)


def product_kernel(counts, n_outs, *refs):
    n_left = sum(counts)
    halves = refs[: counts[0]], refs[counts[0] : n_left]
    right, outs, left = refs[n_left : n_left + 2], refs[n_left + 2 : -1], refs[-1]
    step = pl.program_id(0)
    tokens = right[0].shape[0]

    @pl.when(step == 0)
    def _():
        for half, pieces in enumerate(halves):
            row = 0
            for piece in pieces:
                left[row : row + piece.shape[0], half * tokens : (half + 1) * tokens] = piece[...]
                row += piece.shape[0]

    total = jnp.dot(left[:, :tokens], right[0][...], preferred_element_type=F32)
    total = total + jnp.dot(left[:, tokens:], right[1][...], preferred_element_type=F32)
    chunks = len(outs) // n_outs
    rows = left.shape[0] // n_outs
    each = pl.num_programs(0) // chunks
    for n in range(chunks):

        @pl.when(step // each == n)
        def _(n=n):
            for at in range(n_outs):
                outs[at * chunks + n][...] = total[at * rows : (at + 1) * rows].astype(BF16)


def products(halves, n_outs, rows, chunks):
    tokens, width = rows[0].shape
    n_rows = sum(piece.shape[0] for piece in halves[0])
    tile = 512
    each = width // chunks // tile
    strip = pl.BlockSpec((tokens, tile), lambda i: (0, i))
    outs = pl.pallas_call(
        functools.partial(product_kernel, [len(half) for half in halves], n_outs),
        grid=(width // tile,),
        in_specs=[pl.BlockSpec(p.shape, lambda i: (0, 0)) for half in halves for p in half] + [strip] * 2,
        out_specs=[
            pl.BlockSpec((n_rows // n_outs, tile), lambda i, n=n: (0, jnp.clip(i - n * each, 0, each - 1)))
            for _ in range(n_outs)
            for n in range(chunks)
        ],
        out_shape=[jax.ShapeDtypeStruct((n_rows // n_outs, width // chunks), BF16)] * (n_outs * chunks),
        scratch_shapes=[pltpu.VMEM((n_rows, 2 * tokens), BF16)],
        compiler_params=pltpu.CompilerParams(vmem_limit_bytes=VMEM),
        cost_estimate=SMALL,
    )(*halves[0], *halves[1], *rows)
    return [outs[m * chunks : (m + 1) * chunks] for m in range(n_outs)]


def per_device(acts, cotan, block_ids, basis_in, basis_out, act_factor, grad_factor):
    n_dp = lax.axis_size("dp")
    n_worker = lax.axis_size("worker")
    d = lax.axis_index("dp")
    w = lax.axis_index("worker")
    core, x = d % 2, (d // 2) % 2
    n_z = n_dp // 4
    pool_rows, width = acts.shape
    local_blocks, block_size, _ = basis_in.shape
    model_width = basis_out.shape[0] * block_size
    samples = block_ids.shape[0] * BLK * n_dp
    tokens = pool_rows * n_dp
    rows_dev = model_width // n_dp
    z_per_worker = n_z // n_worker
    cols = width // COL_CHUNKS
    both = ("dp", "worker")

    def swap_core(v):
        return lax.ppermute(v, "dp", [(i, i ^ 1) for i in range(n_dp)])

    def swap_x(v):
        return lax.ppermute(v, "dp", [(i, i ^ 2) for i in range(n_dp)])

    def from_worker(v, step, flip):
        return lax.ppermute(
            v,
            both,
            [
                ((i ^ flip) * n_worker + (j + step) % n_worker, i * n_worker + j)
                for i in range(n_dp)
                for j in range(n_worker)
            ],
        )

    def place(owner, j):
        return owner * z_per_worker + (j if owner < n_worker // 2 else z_per_worker - 1 - j)

    z = d // 4
    starts = list(range(0, width, cols))
    shards = [(step, j) for j in range(z_per_worker) for step in range(n_worker)]

    def hops_of(step, j):
        hops = []
        size = 1
        while size < n_z:
            moves = []
            for i in range(n_worker):
                end = place((i + step) % n_worker, j)
                for low in range(0, n_z, 2 * size):
                    heads = [min(max(end, at), at + size - 1) for at in (low, low + size)]
                    to = min(max(end, low), low + 2 * size - 1)
                    moves.append((i, sum(heads) - to, to))
            hops.append(moves)
            size *= 2
        return hops

    def links(moves):
        found = set()
        for i, a, b in moves:
            ahead = 1 if b > a else -1
            found.update((i, at, at + ahead) for at in range(a, b, ahead))
        return found

    def swap_z(v, bit):
        return lax.ppermute(v, "dp", [(i, i ^ (4 * bit)) for i in range(n_dp)])

    def hop(v, moves):
        pairs = [((a * 4 + r) * n_worker + i, (b * 4 + r) * n_worker + i) for i, a, b in moves for r in range(4)]
        return lax.ppermute(v, both, pairs)

    def piece(j, at, flip):
        part = jnp.where(w < n_worker // 2, j, z_per_worker - 1 - j)
        x_to = x if at else 1 - x
        core_to = 1 - core if flip else core
        return (part * 2 + x_to) * 2 + core_to

    chunks = range(len(starts))
    x_stage, y_stage, z_stage, product_stage, busy = {}, {}, {}, {}, set()
    clock = arrived = 0
    for step, j in shards:
        if step:
            for at in range(2):
                for flip in range(2):
                    y_stage[step, j, at, flip] = arrived + at
            clock = max(clock + 1, arrived + 2)
            product_stage[step, j, 0] = clock - 1
            product_stage[step, j, 1] = max(clock - 1, arrived + 2)
            arrived += 2
        else:
            clock += 1
            product_stage[0, j, 0] = product_stage[0, j, 1] = clock - 1
        for n in chunks:
            x_stage[step, j, n] = clock
    z_bits = [2**bit for bit in range((n_z - 1).bit_length())]
    across = max(clock, 2) + 1
    for n_hop in range(len(z_bits)):
        for step, j, n in x_stage:
            ready = max(x_stage[step, j, n], product_stage[step, j, 1])
            clock = (z_stage[step, j, n, n_hop - 1] if n_hop else ready) + 1
            moves = links(hops_of(step, j)[n_hop])
            while any((clock, link) in busy for link in moves):
                clock += 1
            busy.update((clock, link) for link in moves)
            z_stage[step, j, n, n_hop] = clock
    last = max(*z_stage.values(), across + 1)

    my_start = d * rows_dev
    block = my_start // block_size
    flags = jnp.stack([w * local_blocks, core, x]).astype(jnp.int32)
    env = {"acts": acts, "cotan": cotan}
    done = {}

    def turn(rows, j):
        which = [piece(j, at, flip) for flip in range(2) for at in range(2)]
        *single, both_rows = turned(rows, which, rows_dev)
        found = {("p", j, at, flip): single[2 * flip + at] for flip in range(2) for at in range(2)}
        return {**found, ("p", j): both_rows}

    for stage in range(last + 1):
        if stage:
            keys = sorted(env, key=str)
            env = dict(zip(keys, lax.optimization_barrier(tuple(env[k] for k in keys))))
        joined = {}
        if stage == 0:
            joined["acts_sib"] = swap_core(acts)
            env.update(turn(cotan, 0))
            ours, theirs = pick(acts, cotan, block_ids, core)
            scales = (1.0 / samples, tokens / samples)
            keep, away = terms(flags[1:], ours, swap_core(theirs), block_size, scales)
            away = swap_x(away)
            joined["c", 0] = swap_core(env.pop(("p", 0)))
        if stage == 1:
            for j in range(1, z_per_worker):
                found = turn(env["cotan"], j)
                joined["c", j] = swap_core(found.pop(("p", j)))
                joined.update(found)
        for (step, j, at, flip), when in y_stage.items():
            if when == stage:
                joined["c", step, j, at, flip] = from_worker(env["p", j, at, flip], step, flip)
        for (step, j, n), when in x_stage.items():
            if when == stage:
                joined["got", step, j, n] = swap_x(env.pop(("out", step, j, n)))
        for (step, j, n, at), when in z_stage.items():
            if when == stage:
                joined["hop", step, j, n] = hop(env["acc", step, j, n], hops_of(step, j)[at])

        if stage == 1:
            part = env["keep"].reshape(-1, block_size)
            for far in z_bits:
                bit = z // far % 2
                parts = part.reshape(2, -1, block_size)
                there = lax.dynamic_index_in_dim(parts, 1 - bit, 0, keepdims=False)
                part = lax.dynamic_index_in_dim(parts, bit, 0, keepdims=False) + swap_z(there, far)
            joined["keep"] = part
        if stage == 2:
            part = env["keep"]
            for far in reversed(z_bits):
                other = swap_z(part, far)
                mine_first = jnp.concatenate([part, other], axis=0)
                part = jnp.where(z // far % 2 == 0, mine_first, jnp.concatenate([other, part], axis=0))
            joined["keep"] = part.reshape(local_blocks, -1, block_size)
        if stage == across:
            joined["back"] = swap_x(env["keep"])
            joined["keep_sib"] = swap_core(env["keep"])
        if stage == across + 1:
            back = env.pop("back")
            *done["factors"], eig_in, eig_local = update_factors(
                flags,
                [env.pop("keep"), back, env.pop("keep_sib"), swap_core(back)],
                (act_factor, grad_factor),
                basis_in,
                basis_out,
            )
            eigs = [eig_local] + [from_worker(eig_local, step, 0) for step in range(1, n_worker)]
            eig_out = jnp.concatenate(eigs, axis=0)
            for key in [key for key in env if key[0] == "acc"]:
                env[key], eig_out = lax.optimization_barrier((env[key], eig_out))

        for step, j in shards:
            due = [at for at in range(2) if product_stage[step, j, at] == stage]
            if due:
                known = {**env, **joined} if stage == 0 else env
                if step == 0:
                    halves = [[known["p", j, at, 0] for at in range(2)], [known["c", j]]]
                else:
                    halves = [[known["c", step, j, at, flip] for at in due] for flip in range(2)]
                found = products(halves, len(due), (known["acts"], known["acts_sib"]), len(starts))
                for at, outs in zip(due, found):
                    for n in chunks:
                        joined["mine" if at else "out", step, j, n] = outs[n]
        if stage == 0:
            keep, joined["out", 0, 0, 0] = lax.optimization_barrier((keep, joined["out", 0, 0, 0]))
            joined["keep"] = keep + away
        env.update(joined)
        for step, j, n in x_stage:
            mine, got, acc = ("mine", step, j, n), ("got", step, j, n), ("acc", step, j, n)
            if mine in env and got in env:
                env[acc] = env.pop(mine) + env.pop(got)
            if ("hop", step, j, n) in env:
                env[acc] = env[acc] + env.pop(("hop", step, j, n))
        for n in chunks:
            if stage == max(z_stage[step, j, n, len(z_bits) - 1] for step, j in shards):
                total = None
                for step, j in shards:
                    ends = jnp.array([place((i + step) % n_worker, j) for i in range(n_worker)], jnp.int32)
                    acc = env.pop(("acc", step, j, n))
                    total = acc if total is None else jnp.where(ends[w] == z, acc, total)
                done[n] = total

    act_new, grad_new = done["factors"]
    held = (block // local_blocks - w) % n_worker * local_blocks + block % local_blocks

    sharers = block_size // rows_dev
    spot = jnp.stack([block, d % sharers, held]).astype(jnp.int32)
    precond = None
    for n in range(len(starts)):
        parts = [done[n]]
        for step in range(1, sharers):
            pairs = [(i, i // sharers * sharers + (i + step) % sharers) for i in range(n_dp)]
            parts.append(lax.ppermute(parts[0], "dp", pairs))
        precond = tail(spot, parts, basis_in, basis_out, eig_in, eig_out, n, precond)
    return precond, act_new, grad_new


def solution(mesh):
    return jax.shard_map(
        per_device,
        mesh=mesh,
        in_specs=(
            P("dp", "worker"),
            P("dp", "worker"),
            P("dp"),
            P("worker", None, None),
            P(),
            P("worker", None, None),
            P("worker", None, None),
        ),
        out_specs=(P("dp", "worker"), P("worker", None, None), P("worker", None, None)),
        check_vma=False,
    )
```

```python
import functools

import jax
import jax.numpy as jnp
from jax import lax
from jax.experimental import pallas as pl
from jax.experimental.pallas import tpu as pltpu
from jax.sharding import PartitionSpec as P

BLK = 128
QUARTER = 128
VMEM = 56 * 2**20
COL_CHUNKS = 1


DECAY_RATE = 0.75
DAMPING = 0.03

BF16 = jnp.bfloat16
F32 = jnp.float32

SMALL = pl.CostEstimate(flops=1, bytes_accessed=1, transcendentals=0)


def pick_kernel(n_picks, which_ref, acts, cotan, ours, theirs):
    is_act = which_ref[n_picks] == 0
    ours[...] = jnp.where(is_act, acts[...], cotan[...])
    theirs[...] = jnp.where(is_act, cotan[...], acts[...])


def pick(acts, cotan, block_ids, core):
    n_picks, width = block_ids.shape[0], acts.shape[1]
    chosen = pl.BlockSpec((BLK, width), lambda i, which: (which[i], 0))
    out = pl.BlockSpec((BLK, width), lambda i, which: (i, 0))
    return pl.pallas_call(
        functools.partial(pick_kernel, n_picks),
        grid_spec=pltpu.PrefetchScalarGridSpec(
            num_scalar_prefetch=1, grid=(n_picks,), in_specs=[chosen] * 2, out_specs=[out] * 2
        ),
        out_shape=[jax.ShapeDtypeStruct((n_picks * BLK, width), BF16)] * 2,
        compiler_params=pltpu.CompilerParams(vmem_limit_bytes=VMEM),
        cost_estimate=SMALL,
    )(jnp.concatenate([block_ids, jnp.reshape(core, (1,))]).astype(jnp.int32), acts, cotan)


def pack_upper(full):
    q = QUARTER
    second = jnp.concatenate([full[q : 2 * q, q:], full[3 * q :, 3 * q :]], axis=1)
    third = full[2 * q : 3 * q, 2 * q :]
    third = jnp.concatenate([third[: q // 2], third[q // 2 :]], axis=1)
    return jnp.concatenate([full[:q], second, third], axis=0)


def term_kernel(scales, place_ref, ours, theirs, keep, away):
    total = 0.0
    for rows in (ours[...], theirs[...]):
        total = total + lax.dot_general(
            rows, rows, (((0,), (0,)), ((), ())), preferred_element_type=F32
        )
    scale = jnp.where(place_ref[0] == 0, scales[0], scales[1]).astype(F32)
    packed = pack_upper(total * scale)
    half = packed.shape[0] // 2
    low = place_ref[1] == 0
    keep[0] = jnp.where(low, packed[:half], packed[half:]).astype(BF16)
    away[0] = jnp.where(low, packed[half:], packed[:half]).astype(BF16)


def terms(place, ours, theirs, size, scales):
    rows, width = ours.shape
    blocks, half = width // size, 5 * QUARTER // 4
    strip = pl.BlockSpec((rows, size), lambda b, place: (0, b))
    out = pl.BlockSpec((1, half, size), lambda b, place: (b, 0, 0))
    return pl.pallas_call(
        functools.partial(term_kernel, scales),
        grid_spec=pltpu.PrefetchScalarGridSpec(
            num_scalar_prefetch=1, grid=(blocks,), in_specs=[strip] * 2, out_specs=[out] * 2
        ),
        out_shape=[jax.ShapeDtypeStruct((blocks, half, size), BF16)] * 2,
        compiler_params=pltpu.CompilerParams(vmem_limit_bytes=VMEM),
        cost_estimate=SMALL,
    )(place, ours, theirs)


def unpack_upper(packed):
    q = QUARTER
    tiles = {}
    for j in range(4):
        tiles[0, j] = packed[:q, j * q : (j + 1) * q]
    for j in range(1, 4):
        tiles[1, j] = packed[q : 2 * q, (j - 1) * q : j * q]
    tiles[3, 3] = packed[q : 2 * q, 3 * q :]
    third = jnp.concatenate([packed[2 * q :, : 2 * q], packed[2 * q :, 2 * q :]], axis=0)
    tiles[2, 2], tiles[2, 3] = third[:, :q], third[:, q:]
    return [[tiles[i, j] if j >= i else tiles[j, i].T for j in range(4)] for i in range(4)]


def factor_kernel(place_ref, keep, back, keep_sib, back_sib, *refs):
    low = place_ref[2] == 0
    for kind, (factor, basis, new, eig) in enumerate(zip(refs[0:2], refs[2:4], refs[4:6], refs[6:8])):
        here = place_ref[1] == kind
        kept = jnp.where(here, keep[0], keep_sib[0])
        came = jnp.where(here, back[0], back_sib[0])
        halves = [jnp.where(low, kept, came), jnp.where(low, came, kept)]
        rows = unpack_upper(jnp.concatenate(halves, axis=0).astype(F32))
        q = QUARTER
        for i in range(4):
            for j in range(4):
                at = (0, pl.ds(i * q, q), pl.ds(j * q, q))
                new[at] = DECAY_RATE * factor[at] + (1.0 - DECAY_RATE) * rows[i][j]
        vectors = basis[0]
        rest = new[0]
        product = 0.0
        for _ in range(3):
            part = rest.astype(BF16)
            rest = rest - part.astype(F32)
            product = product + jnp.dot(part, vectors, preferred_element_type=F32)
        eig[0] = jnp.sum(vectors.astype(F32) * product, axis=0, keepdims=True)


def update_factors(place, halves, factors, basis_in, basis_out):
    blocks, size, _ = basis_in.shape

    def local(b, place):
        return (b, 0, 0)

    square = pl.BlockSpec((1, size, size), local)
    narrow = pl.BlockSpec((1, halves[0].shape[1], size), local)
    line = pl.BlockSpec((1, 1, size), local)
    return pl.pallas_call(
        factor_kernel,
        grid_spec=pltpu.PrefetchScalarGridSpec(
            num_scalar_prefetch=1,
            grid=(blocks,),
            in_specs=[narrow] * 4
            + [square] * 3
            + [pl.BlockSpec((1, size, size), lambda b, place: (place[0] + b, 0, 0))],
            out_specs=[square, square, line, line],
        ),
        out_shape=[jax.ShapeDtypeStruct((blocks, size, size), F32)] * 2
        + [jax.ShapeDtypeStruct((blocks, 1, size), F32)] * 2,
        compiler_params=pltpu.CompilerParams(vmem_limit_bytes=VMEM),
        cost_estimate=SMALL,
    )(place, *halves, *factors, basis_in, basis_out)


def tail_kernel(n_parts, place_ref, *refs):
    parts, (basis, outer, eig_in, eig_out) = refs[:n_parts], refs[n_parts : n_parts + 4]
    out, whole = refs[-2:]
    sharers = len(parts)
    rows = parts[0].shape[0]
    me = place_ref[1]
    for step, part in enumerate(parts):
        spot = lax.rem(me - step + sharers, sharers)
        whole[pl.ds(pl.multiple_of(spot * rows, rows), rows), :] = part[...]
    right = jnp.dot(whole[...], basis[0], preferred_element_type=F32).astype(BF16)
    inner = lax.dot_general(outer[0], right, (((0,), (0,)), ((), ())), preferred_element_type=F32)
    column = jnp.broadcast_to(eig_out[0], (QUARTER, eig_out.shape[2])).T[:, :1]
    scaled = (inner / (column * eig_in[0] + DAMPING)).astype(BF16)
    mine = outer[0, pl.ds(pl.multiple_of(me * rows, rows), rows), :]
    upper = jnp.dot(mine, scaled, preferred_element_type=F32).astype(BF16)
    out[...] = lax.dot_general(
        upper, basis[0], (((1,), (1,)), ((), ())), preferred_element_type=F32
    ).astype(BF16)


def tail(place, parts, basis_in, basis_out, eig_in, eig_out, chunk, filled):
    blocks, size, _ = basis_in.shape
    rows, cols = parts[0].shape
    each = cols // size
    strip = pl.BlockSpec((rows, size), lambda b, place: (0, b))
    in_specs = [strip] * len(parts) + [
        pl.BlockSpec((1, size, size), lambda b, place: (chunk * each + b, 0, 0)),
        pl.BlockSpec((1, size, size), lambda b, place: (place[0], 0, 0)),
        pl.BlockSpec((1, 1, size), lambda b, place: (chunk * each + b, 0, 0)),
        pl.BlockSpec((1, 1, size), lambda b, place: (place[2], 0, 0)),
    ]
    args = [place, *parts, basis_in, basis_out, eig_in, eig_out]
    aliases = {}
    if filled is not None:
        in_specs.append(pl.BlockSpec(memory_space=pl.ANY))
        aliases = {len(args): 0}
        args.append(filled)
    return pl.pallas_call(
        functools.partial(tail_kernel, len(parts)),
        grid_spec=pltpu.PrefetchScalarGridSpec(
            num_scalar_prefetch=1,
            grid=(each,),
            in_specs=in_specs,
            out_specs=pl.BlockSpec((rows, size), lambda b, place: (0, chunk * each + b)),
            scratch_shapes=[pltpu.VMEM((size, size), BF16)],
        ),
        out_shape=jax.ShapeDtypeStruct((rows, blocks * size), BF16),
        input_output_aliases=aliases,
        compiler_params=pltpu.CompilerParams(vmem_limit_bytes=VMEM),
        cost_estimate=pl.CostEstimate(
            flops=each * 6 * size**3, bytes_accessed=4 * each * size**2, transcendentals=0
        ),
    )(*args)


def turn_kernel(which_ref, block, first, second, across):
    del which_ref
    step = pl.program_id(0)
    flipped = block[...].T

    @pl.when(step < 2)
    def _():
        first[...] = flipped

    @pl.when(step >= 2)
    def _():
        second[...] = flipped

    @pl.when(step % 2 == 1)
    def _():
        across[...] = flipped


def turned(rows, which, n_rows):
    tokens, _ = rows.shape

    def out(place):
        return pl.BlockSpec((n_rows, tokens), lambda i, which: (place(i), 0))

    return pl.pallas_call(
        turn_kernel,
        grid_spec=pltpu.PrefetchScalarGridSpec(
            num_scalar_prefetch=1,
            grid=(4,),
            in_specs=[pl.BlockSpec((tokens, n_rows), lambda i, which: (0, which[i]))],
            out_specs=[
                out(lambda i: jnp.minimum(i, 1)),
                out(lambda i: jnp.maximum(i - 2, 0)),
                out(lambda i: i // 2),
            ],
        ),
        out_shape=[jax.ShapeDtypeStruct((2 * n_rows, tokens), BF16)] * 3,
        compiler_params=pltpu.CompilerParams(vmem_limit_bytes=VMEM),
        cost_estimate=SMALL,
    )(jnp.stack(which).astype(jnp.int32), rows)


def product_kernel(counts, n_outs, *refs):
    n_left = sum(counts)
    halves = refs[: counts[0]], refs[counts[0] : n_left]
    right, outs, left = refs[n_left : n_left + 2], refs[n_left + 2 : -1], refs[-1]
    step = pl.program_id(0)
    tokens = right[0].shape[0]

    @pl.when(step == 0)
    def _():
        for half, pieces in enumerate(halves):
            row = 0
            for piece in pieces:
                left[row : row + piece.shape[0], half * tokens : (half + 1) * tokens] = piece[...]
                row += piece.shape[0]

    total = jnp.dot(left[:, :tokens], right[0][...], preferred_element_type=F32)
    total = total + jnp.dot(left[:, tokens:], right[1][...], preferred_element_type=F32)
    chunks = len(outs) // n_outs
    rows = left.shape[0] // n_outs
    each = pl.num_programs(0) // chunks
    for n in range(chunks):

        @pl.when(step // each == n)
        def _(n=n):
            for at in range(n_outs):
                outs[at * chunks + n][...] = total[at * rows : (at + 1) * rows].astype(BF16)


def products(halves, n_outs, n_rows, rows, chunks):
    tokens, width = rows[0].shape
    tile = 512
    each = width // chunks // tile
    strip = pl.BlockSpec((tokens, tile), lambda i: (0, i))
    first, second = ([min(p.shape[0], n_rows * n_outs // len(half)) for p in half] for half in halves)
    outs = pl.pallas_call(
        functools.partial(product_kernel, [len(half) for half in halves], n_outs),
        grid=(width // tile,),
        in_specs=[pl.BlockSpec((size, tokens), lambda i: (0, 0)) for size in first + second] + [strip] * 2,
        out_specs=[
            pl.BlockSpec((n_rows, tile), lambda i, n=n: (0, jnp.clip(i - n * each, 0, each - 1)))
            for _ in range(n_outs)
            for n in range(chunks)
        ],
        out_shape=[jax.ShapeDtypeStruct((n_rows, width // chunks), BF16)] * (n_outs * chunks),
        scratch_shapes=[pltpu.VMEM((n_outs * n_rows, 2 * tokens), BF16)],
        compiler_params=pltpu.CompilerParams(vmem_limit_bytes=VMEM),
        cost_estimate=pl.CostEstimate(
            flops=8 * n_outs * tokens * n_rows * width, bytes_accessed=4 * tokens * width, transcendentals=0
        ),
    )(*halves[0], *halves[1], *rows)
    return [outs[m * chunks : (m + 1) * chunks] for m in range(n_outs)]


def per_device(acts, cotan, block_ids, basis_in, basis_out, act_factor, grad_factor):
    n_dp = lax.axis_size("dp")
    n_worker = lax.axis_size("worker")
    d = lax.axis_index("dp")
    w = lax.axis_index("worker")
    core, x = d % 2, (d // 2) % 2
    n_z = n_dp // 4
    pool_rows, width = acts.shape
    local_blocks, block_size, _ = basis_in.shape
    model_width = basis_out.shape[0] * block_size
    samples = block_ids.shape[0] * BLK * n_dp
    tokens = pool_rows * n_dp
    rows_dev = model_width // n_dp
    z_per_worker = n_z // n_worker
    cols = width // COL_CHUNKS
    both = ("dp", "worker")

    def swap_core(v):
        return lax.ppermute(v, "dp", [(i, i ^ 1) for i in range(n_dp)])

    def swap_x(v):
        return lax.ppermute(v, "dp", [(i, i ^ 2) for i in range(n_dp)])

    def from_worker(v, step):
        return lax.ppermute(v, "worker", [((j + step) % n_worker, j) for j in range(n_worker)])

    def place(owner, j):
        return owner * z_per_worker + (j if owner < n_worker // 2 else z_per_worker - 1 - j)

    z = d // 4
    starts = list(range(0, width, cols))
    shards = [(step, j) for j in range(z_per_worker) for step in range(n_worker)]

    def hops_of(step, j):
        hops = []
        size = 1
        while size < n_z:
            moves = []
            for i in range(n_worker):
                end = place((i + step) % n_worker, j)
                for low in range(0, n_z, 2 * size):
                    heads = [min(max(end, at), at + size - 1) for at in (low, low + size)]
                    to = min(max(end, low), low + 2 * size - 1)
                    moves.append((i, sum(heads) - to, to))
            hops.append(moves)
            size *= 2
        return hops

    def links(moves):
        found = set()
        for i, a, b in moves:
            ahead = 1 if b > a else -1
            found.update((i, at, at + ahead) for at in range(a, b, ahead))
        return found

    def swap_z(v, bit):
        return lax.ppermute(v, "dp", [(i, i ^ (4 * bit)) for i in range(n_dp)])

    def hop(v, moves):
        pairs = [((a * 4 + r) * n_worker + i, (b * 4 + r) * n_worker + i) for i, a, b in moves for r in range(4)]
        return lax.ppermute(v, both, pairs)

    def piece(j, at, flip):
        part = jnp.where(w < n_worker // 2, j, z_per_worker - 1 - j)
        x_to = x if at else 1 - x
        core_to = 1 - core if flip else core
        return (part * 2 + x_to) * 2 + core_to

    chunks = range(len(starts))
    x_stage, y_stage, z_stage, product_stage, busy = {}, {}, {}, {}, set()
    clock = arrived = 0
    for step, j in shards:
        if step:
            for at in range(2):
                y_stage[step, j, at] = arrived + at
            clock = max(clock + 1, arrived + 2)
            product_stage[step, j, 0] = clock - 1
            product_stage[step, j, 1] = max(clock - 1, arrived + 2)
            arrived += 2
        else:
            clock += 1
            product_stage[0, j, 0] = product_stage[0, j, 1] = clock - 1
        for n in chunks:
            x_stage[step, j, n] = clock
    z_bits = [2**bit for bit in range((n_z - 1).bit_length())]
    across = max(clock, 2) + 1
    for n_hop in range(len(z_bits)):
        for step, j, n in x_stage:
            ready = max(x_stage[step, j, n], product_stage[step, j, 1])
            clock = (z_stage[step, j, n, n_hop - 1] if n_hop else max(ready, 2)) + 1
            moves = links(hops_of(step, j)[n_hop])
            while any((clock, link) in busy for link in moves):
                clock += 1
            busy.update((clock, link) for link in moves)
            z_stage[step, j, n, n_hop] = clock
    last = max(*z_stage.values(), across + 1)

    my_start = d * rows_dev
    block = my_start // block_size
    flags = jnp.stack([w * local_blocks, core, x]).astype(jnp.int32)
    env = {"acts": acts, "cotan": cotan}
    done = {}

    def turn(rows, j):
        which = [piece(j, at, flip) for at in range(2) for flip in range(2)]
        other, own, across = turned(rows, which, rows_dev)
        return {("p", j, 0): other, ("p", j, 1): own, ("p", j): across}

    def gathered(part, bits):
        for far in bits:
            other = swap_z(part, far)
            mine_first = jnp.concatenate([part, other], axis=0)
            part = jnp.where(z // far % 2 == 0, mine_first, jnp.concatenate([other, part], axis=0))
        return part

    for stage in range(last + 1):
        if stage:
            keys = sorted(env, key=str)
            env = dict(zip(keys, lax.optimization_barrier(tuple(env[k] for k in keys))))
        joined = {}
        if stage == 0:
            joined["acts_sib"] = swap_core(acts)
            env.update(turn(cotan, 0))
            ours, theirs = pick(acts, cotan, block_ids, core)
            scales = (1.0 / samples, tokens / samples)
            keep, away = terms(flags[1:], ours, swap_core(theirs), block_size, scales)
            away = swap_x(away)
            joined["c", 0] = swap_core(env.pop(("p", 0)))
        if stage == 1:
            for j in range(1, z_per_worker):
                found = turn(env["cotan"], j)
                joined["c", j] = swap_core(found.pop(("p", j)))
                joined.update(found)
        arrivals = {}
        for (step, j, at), when in y_stage.items():
            if when == stage:
                joined["r", step, j, at] = from_worker(env["p", j, at], step)
            if when == stage - 1:
                arrivals[step, j, at] = swap_core(env["r", step, j, at][rows_dev:])
        for (step, j, n), when in x_stage.items():
            if when == stage:
                joined["got", step, j, n] = swap_x(env.pop(("out", step, j, n)))
        for (step, j, n, at), when in z_stage.items():
            if when == stage:
                joined["hop", step, j, n] = hop(env["acc", step, j, n], hops_of(step, j)[at])

        if stage == 1:
            part = env["keep"].reshape(-1, block_size)
            for far in z_bits:
                bit = z // far % 2
                parts = part.reshape(2, -1, block_size)
                there = lax.dynamic_index_in_dim(parts, 1 - bit, 0, keepdims=False)
                part = lax.dynamic_index_in_dim(parts, bit, 0, keepdims=False) + swap_z(there, far)
            joined["keep"] = gathered(part, z_bits[-1:])
        if stage == 2:
            part = gathered(env["keep"], reversed(z_bits[:-1]))
            joined["keep"] = part.reshape(local_blocks, -1, block_size)
        if stage == across:
            joined["back"] = swap_x(env["keep"])
            joined["keep_sib"] = swap_core(env["keep"])
        if stage == across + 1:
            back = env.pop("back")
            *done["factors"], eig_in, eig_local = update_factors(
                flags,
                [env.pop("keep"), back, env.pop("keep_sib"), swap_core(back)],
                (act_factor, grad_factor),
                basis_in,
                basis_out,
            )
            eigs = [eig_local] + [from_worker(eig_local, step) for step in range(1, n_worker)]
            eig_out = jnp.concatenate(eigs, axis=0)
            for key in [key for key in env if key[0] == "acc"]:
                env[key], eig_out = lax.optimization_barrier((env[key], eig_out))

        for (step, j, at), rows in arrivals.items():
            joined["s", step, j, at] = rows
        for step, j in shards:
            due = [at for at in range(2) if product_stage[step, j, at] == stage]
            if due:
                known = {**env, **joined} if stage == 0 else {**env, **{("s", *k): v for k, v in arrivals.items()}}
                if step == 0:
                    halves = [[known["p", j, at] for at in range(2)], [known["c", j]]]
                else:
                    halves = [[known[name, step, j, at] for at in due] for name in ("r", "s")]
                found = products(halves, len(due), rows_dev, (known["acts"], known["acts_sib"]), len(starts))
                for at, outs in zip(due, found):
                    for n in chunks:
                        joined["mine" if at else "out", step, j, n] = outs[n]
        if stage == 0:
            keep, joined["out", 0, 0, 0] = lax.optimization_barrier((keep, joined["out", 0, 0, 0]))
            joined["keep"] = keep + away
        env.update(joined)
        for step, j, n in x_stage:
            mine, got, acc = ("mine", step, j, n), ("got", step, j, n), ("acc", step, j, n)
            if mine in env and got in env:
                env[acc] = env.pop(mine) + env.pop(got)
            if ("hop", step, j, n) in env:
                env[acc] = env[acc] + env.pop(("hop", step, j, n))
        for n in chunks:
            if stage == max(z_stage[step, j, n, len(z_bits) - 1] for step, j in shards):
                total = None
                for step, j in shards:
                    ends = jnp.array([place((i + step) % n_worker, j) for i in range(n_worker)], jnp.int32)
                    acc = env.pop(("acc", step, j, n))
                    total = acc if total is None else jnp.where(ends[w] == z, acc, total)
                done[n] = total

    act_new, grad_new = done["factors"]
    held = (block // local_blocks - w) % n_worker * local_blocks + block % local_blocks

    sharers = block_size // rows_dev
    spot = jnp.stack([block, d % sharers, held]).astype(jnp.int32)
    precond = None
    for n in range(len(starts)):
        parts = [done[n]]
        for step in range(1, sharers):
            pairs = [(i, i // sharers * sharers + (i + step) % sharers) for i in range(n_dp)]
            parts.append(lax.ppermute(parts[0], "dp", pairs))
        precond = tail(spot, parts, basis_in, basis_out, eig_in, eig_out, n, precond)
    return precond, act_new, grad_new


def solution(mesh):
    return jax.shard_map(
        per_device,
        mesh=mesh,
        in_specs=(
            P("dp", "worker"),
            P("dp", "worker"),
            P("dp"),
            P("worker", None, None),
            P(),
            P("worker", None, None),
            P("worker", None, None),
        ),
        out_specs=(P("dp", "worker"), P("worker", None, None), P("worker", None, None)),
        check_vma=False,
    )
```

```python
import functools

import jax
import jax.numpy as jnp
from jax import lax
from jax.experimental import pallas as pl
from jax.experimental.pallas import tpu as pltpu
from jax.sharding import PartitionSpec as P

BLK = 128
QUARTER = 128
VMEM = 56 * 2**20
COL_CHUNKS = 1


DECAY_RATE = 0.75
DAMPING = 0.03

BF16 = jnp.bfloat16
F32 = jnp.float32

SMALL = pl.CostEstimate(flops=1, bytes_accessed=1, transcendentals=0)


def pick_kernel(n_picks, which_ref, acts, cotan, ours, theirs):
    is_act = which_ref[n_picks] == 0
    ours[...] = jnp.where(is_act, acts[...], cotan[...])
    theirs[...] = jnp.where(is_act, cotan[...], acts[...])


def pick(acts, cotan, block_ids, core):
    n_picks, width = block_ids.shape[0], acts.shape[1]
    chosen = pl.BlockSpec((BLK, width), lambda i, which: (which[i], 0))
    out = pl.BlockSpec((BLK, width), lambda i, which: (i, 0))
    return pl.pallas_call(
        functools.partial(pick_kernel, n_picks),
        grid_spec=pltpu.PrefetchScalarGridSpec(
            num_scalar_prefetch=1, grid=(n_picks,), in_specs=[chosen] * 2, out_specs=[out] * 2
        ),
        out_shape=[jax.ShapeDtypeStruct((n_picks * BLK, width), BF16)] * 2,
        compiler_params=pltpu.CompilerParams(vmem_limit_bytes=VMEM),
        cost_estimate=SMALL,
    )(jnp.concatenate([block_ids, jnp.reshape(core, (1,))]).astype(jnp.int32), acts, cotan)


def pack_upper(full):
    q = QUARTER
    second = jnp.concatenate([full[q : 2 * q, q:], full[3 * q :, 3 * q :]], axis=1)
    third = full[2 * q : 3 * q, 2 * q :]
    third = jnp.concatenate([third[: q // 2], third[q // 2 :]], axis=1)
    return jnp.concatenate([full[:q], second, third], axis=0)


def term_kernel(scales, place_ref, ours, theirs, keep, away):
    total = 0.0
    for rows in (ours[...], theirs[...]):
        total = total + lax.dot_general(
            rows, rows, (((0,), (0,)), ((), ())), preferred_element_type=F32
        )
    scale = jnp.where(place_ref[0] == 0, scales[0], scales[1]).astype(F32)
    packed = pack_upper(total * scale)
    half = packed.shape[0] // 2
    low = place_ref[1] == 0
    keep[0] = jnp.where(low, packed[:half], packed[half:]).astype(BF16)
    away[0] = jnp.where(low, packed[half:], packed[:half]).astype(BF16)


def terms(place, ours, theirs, size, scales):
    rows, width = ours.shape
    blocks, half = width // size, 5 * QUARTER // 4
    strip = pl.BlockSpec((rows, size), lambda b, place: (0, b))
    out = pl.BlockSpec((1, half, size), lambda b, place: (b, 0, 0))
    return pl.pallas_call(
        functools.partial(term_kernel, scales),
        grid_spec=pltpu.PrefetchScalarGridSpec(
            num_scalar_prefetch=1, grid=(blocks,), in_specs=[strip] * 2, out_specs=[out] * 2
        ),
        out_shape=[jax.ShapeDtypeStruct((blocks, half, size), BF16)] * 2,
        compiler_params=pltpu.CompilerParams(vmem_limit_bytes=VMEM),
        cost_estimate=SMALL,
    )(place, ours, theirs)


def unpack_upper(packed):
    q = QUARTER
    tiles = {}
    for j in range(4):
        tiles[0, j] = packed[:q, j * q : (j + 1) * q]
    for j in range(1, 4):
        tiles[1, j] = packed[q : 2 * q, (j - 1) * q : j * q]
    tiles[3, 3] = packed[q : 2 * q, 3 * q :]
    third = jnp.concatenate([packed[2 * q :, : 2 * q], packed[2 * q :, 2 * q :]], axis=0)
    tiles[2, 2], tiles[2, 3] = third[:, :q], third[:, q:]
    return [[tiles[i, j] if j >= i else tiles[j, i].T for j in range(4)] for i in range(4)]


def factor_kernel(place_ref, keep, back, keep_sib, back_sib, *refs):
    low = place_ref[2] == 0
    for kind, (factor, basis, new, eig) in enumerate(zip(refs[0:2], refs[2:4], refs[4:6], refs[6:8])):
        here = place_ref[1] == kind
        kept = jnp.where(here, keep[0], keep_sib[0])
        came = jnp.where(here, back[0], back_sib[0])
        halves = [jnp.where(low, kept, came), jnp.where(low, came, kept)]
        rows = unpack_upper(jnp.concatenate(halves, axis=0).astype(F32))
        q = QUARTER
        for i in range(4):
            for j in range(4):
                at = (0, pl.ds(i * q, q), pl.ds(j * q, q))
                new[at] = DECAY_RATE * factor[at] + (1.0 - DECAY_RATE) * rows[i][j]
        vectors = basis[0]
        rest = new[0]
        product = 0.0
        for _ in range(3):
            part = rest.astype(BF16)
            rest = rest - part.astype(F32)
            product = product + jnp.dot(part, vectors, preferred_element_type=F32)
        eig[0] = jnp.sum(vectors.astype(F32) * product, axis=0, keepdims=True)


def update_factors(place, halves, factors, basis_in, basis_out):
    blocks, size, _ = basis_in.shape

    def local(b, place):
        return (b, 0, 0)

    square = pl.BlockSpec((1, size, size), local)
    narrow = pl.BlockSpec((1, halves[0].shape[1], size), local)
    line = pl.BlockSpec((1, 1, size), local)
    return pl.pallas_call(
        factor_kernel,
        grid_spec=pltpu.PrefetchScalarGridSpec(
            num_scalar_prefetch=1,
            grid=(blocks,),
            in_specs=[narrow] * 4
            + [square] * 3
            + [pl.BlockSpec((1, size, size), lambda b, place: (place[0] + b, 0, 0))],
            out_specs=[square, square, line, line],
        ),
        out_shape=[jax.ShapeDtypeStruct((blocks, size, size), F32)] * 2
        + [jax.ShapeDtypeStruct((blocks, 1, size), F32)] * 2,
        compiler_params=pltpu.CompilerParams(vmem_limit_bytes=VMEM),
        cost_estimate=SMALL,
    )(place, *halves, *factors, basis_in, basis_out)


def tail_kernel(n_parts, place_ref, *refs):
    parts, (basis, outer, eig_in, eig_out) = refs[:n_parts], refs[n_parts : n_parts + 4]
    out, whole = refs[-2:]
    sharers = len(parts)
    rows = parts[0].shape[0]
    me = place_ref[1]
    size = whole.shape[1]
    columns = pl.ds(pl.multiple_of(pl.program_id(0) * size, size), size)
    for step, part in enumerate(parts):
        spot = lax.rem(me - step + sharers, sharers)
        whole[pl.ds(pl.multiple_of(spot * rows, rows), rows), :] = part[:, columns]
    right = jnp.dot(whole[...], basis[0], preferred_element_type=F32).astype(BF16)
    inner = lax.dot_general(outer[0], right, (((0,), (0,)), ((), ())), preferred_element_type=F32)
    column = jnp.broadcast_to(eig_out[0], (QUARTER, eig_out.shape[2])).T[:, :1]
    scaled = (inner / (column * eig_in[0] + DAMPING)).astype(BF16)
    mine = outer[0, pl.ds(pl.multiple_of(me * rows, rows), rows), :]
    upper = jnp.dot(mine, scaled, preferred_element_type=F32).astype(BF16)
    out[...] = lax.dot_general(
        upper, basis[0], (((1,), (1,)), ((), ())), preferred_element_type=F32
    ).astype(BF16)


def tail(place, parts, basis_in, basis_out, eig_in, eig_out, chunk, filled):
    blocks, size, _ = basis_in.shape
    rows, cols = parts[0].shape
    each = cols // size
    in_specs = [pl.BlockSpec(memory_space=pltpu.VMEM)] * len(parts) + [
        pl.BlockSpec((1, size, size), lambda b, place: (chunk * each + b, 0, 0)),
        pl.BlockSpec((1, size, size), lambda b, place: (place[0], 0, 0)),
        pl.BlockSpec((1, 1, size), lambda b, place: (chunk * each + b, 0, 0)),
        pl.BlockSpec((1, 1, size), lambda b, place: (place[2], 0, 0)),
    ]
    args = [place, *parts, basis_in, basis_out, eig_in, eig_out]
    aliases = {}
    if filled is not None:
        in_specs.append(pl.BlockSpec(memory_space=pl.ANY))
        aliases = {len(args): 0}
        args.append(filled)
    return pl.pallas_call(
        functools.partial(tail_kernel, len(parts)),
        grid_spec=pltpu.PrefetchScalarGridSpec(
            num_scalar_prefetch=1,
            grid=(each,),
            in_specs=in_specs,
            out_specs=pl.BlockSpec((rows, size), lambda b, place: (0, chunk * each + b)),
            scratch_shapes=[pltpu.VMEM((size, size), BF16)],
        ),
        out_shape=jax.ShapeDtypeStruct((rows, blocks * size), BF16),
        input_output_aliases=aliases,
        compiler_params=pltpu.CompilerParams(vmem_limit_bytes=VMEM),
        cost_estimate=pl.CostEstimate(
            flops=each * 6 * size**3, bytes_accessed=4 * each * size**2, transcendentals=0
        ),
    )(*args)


def turn_kernel(which_ref, block, first, second, across):
    del which_ref
    step = pl.program_id(0)
    flipped = block[...].T

    @pl.when(step < 2)
    def _():
        first[...] = flipped

    @pl.when(step >= 2)
    def _():
        second[...] = flipped

    @pl.when(step % 2 == 1)
    def _():
        across[...] = flipped


def turned(rows, which, n_rows):
    tokens, _ = rows.shape

    def out(place):
        return pl.BlockSpec((n_rows, tokens), lambda i, which: (place(i), 0))

    return pl.pallas_call(
        turn_kernel,
        grid_spec=pltpu.PrefetchScalarGridSpec(
            num_scalar_prefetch=1,
            grid=(4,),
            in_specs=[pl.BlockSpec((tokens, n_rows), lambda i, which: (0, which[i]))],
            out_specs=[
                out(lambda i: jnp.minimum(i, 1)),
                out(lambda i: jnp.maximum(i - 2, 0)),
                out(lambda i: i // 2),
            ],
        ),
        out_shape=[jax.ShapeDtypeStruct((2 * n_rows, tokens), BF16)] * 3,
        compiler_params=pltpu.CompilerParams(vmem_limit_bytes=VMEM),
        cost_estimate=SMALL,
    )(jnp.stack(which).astype(jnp.int32), rows)


def product_kernel(counts, n_outs, *refs):
    n_left = sum(counts)
    halves = refs[: counts[0]], refs[counts[0] : n_left]
    right, outs, left = refs[n_left : n_left + 2], refs[n_left + 2 : -1], refs[-1]
    step = pl.program_id(0)
    tokens = right[0].shape[0]

    @pl.when(step == 0)
    def _():
        for half, pieces in enumerate(halves):
            row = 0
            for piece in pieces:
                left[row : row + piece.shape[0], half * tokens : (half + 1) * tokens] = piece[...]
                row += piece.shape[0]

    total = jnp.dot(left[:, :tokens], right[0][...], preferred_element_type=F32)
    total = total + jnp.dot(left[:, tokens:], right[1][...], preferred_element_type=F32)
    chunks = len(outs) // n_outs
    rows = left.shape[0] // n_outs
    each = pl.num_programs(0) // chunks
    for n in range(chunks):

        @pl.when(step // each == n)
        def _(n=n):
            for at in range(n_outs):
                outs[at * chunks + n][...] = total[at * rows : (at + 1) * rows].astype(BF16)


def products(halves, n_outs, n_rows, rows, chunks):
    tokens, width = rows[0].shape
    tile = 512
    each = width // chunks // tile
    strip = pl.BlockSpec((tokens, tile), lambda i: (0, i))
    first, second = ([min(p.shape[0], n_rows * n_outs // len(half)) for p in half] for half in halves)
    outs = pl.pallas_call(
        functools.partial(product_kernel, [len(half) for half in halves], n_outs),
        grid=(width // tile,),
        in_specs=[pl.BlockSpec((size, tokens), lambda i: (0, 0)) for size in first + second] + [strip] * 2,
        out_specs=[
            pl.BlockSpec((n_rows, tile), lambda i, n=n: (0, jnp.clip(i - n * each, 0, each - 1)))
            for _ in range(n_outs)
            for n in range(chunks)
        ],
        out_shape=[jax.ShapeDtypeStruct((n_rows, width // chunks), BF16)] * (n_outs * chunks),
        scratch_shapes=[pltpu.VMEM((n_outs * n_rows, 2 * tokens), BF16)],
        compiler_params=pltpu.CompilerParams(vmem_limit_bytes=VMEM),
        cost_estimate=pl.CostEstimate(
            flops=8 * n_outs * tokens * n_rows * width, bytes_accessed=4 * tokens * width, transcendentals=0
        ),
    )(*halves[0], *halves[1], *rows)
    return [outs[m * chunks : (m + 1) * chunks] for m in range(n_outs)]


def per_device(acts, cotan, block_ids, basis_in, basis_out, act_factor, grad_factor):
    n_dp = lax.axis_size("dp")
    n_worker = lax.axis_size("worker")
    d = lax.axis_index("dp")
    w = lax.axis_index("worker")
    core, x = d % 2, (d // 2) % 2
    n_z = n_dp // 4
    pool_rows, width = acts.shape
    local_blocks, block_size, _ = basis_in.shape
    model_width = basis_out.shape[0] * block_size
    samples = block_ids.shape[0] * BLK * n_dp
    tokens = pool_rows * n_dp
    rows_dev = model_width // n_dp
    z_per_worker = n_z // n_worker
    cols = width // COL_CHUNKS
    both = ("dp", "worker")

    def swap_core(v):
        return lax.ppermute(v, "dp", [(i, i ^ 1) for i in range(n_dp)])

    def swap_x(v):
        return lax.ppermute(v, "dp", [(i, i ^ 2) for i in range(n_dp)])

    def from_worker(v, step):
        return lax.ppermute(v, "worker", [((j + step) % n_worker, j) for j in range(n_worker)])

    def place(owner, j):
        return owner * z_per_worker + (j if owner < n_worker // 2 else z_per_worker - 1 - j)

    z = d // 4
    starts = list(range(0, width, cols))
    shards = [(step, j) for j in range(z_per_worker) for step in range(n_worker)]

    def hops_of(step, j):
        hops = []
        size = 1
        while size < n_z:
            moves = []
            for i in range(n_worker):
                end = place((i + step) % n_worker, j)
                for low in range(0, n_z, 2 * size):
                    heads = [min(max(end, at), at + size - 1) for at in (low, low + size)]
                    to = min(max(end, low), low + 2 * size - 1)
                    moves.append((i, sum(heads) - to, to))
            hops.append(moves)
            size *= 2
        return hops

    def links(moves):
        found = set()
        for i, a, b in moves:
            ahead = 1 if b > a else -1
            found.update((i, at, at + ahead) for at in range(a, b, ahead))
        return found

    def swap_z(v, bit):
        return lax.ppermute(v, "dp", [(i, i ^ (4 * bit)) for i in range(n_dp)])

    def hop(v, moves):
        pairs = [((a * 4 + r) * n_worker + i, (b * 4 + r) * n_worker + i) for i, a, b in moves for r in range(4)]
        return lax.ppermute(v, both, pairs)

    def piece(j, at, flip):
        part = jnp.where(w < n_worker // 2, j, z_per_worker - 1 - j)
        x_to = x if at else 1 - x
        core_to = 1 - core if flip else core
        return (part * 2 + x_to) * 2 + core_to

    chunks = range(len(starts))
    x_stage, y_stage, z_stage, product_stage, busy = {}, {}, {}, {}, set()
    clock = arrived = 0
    for step, j in shards:
        if step:
            for at in range(2):
                y_stage[step, j, at] = arrived + at
            clock = max(clock + 1, arrived + 2)
            product_stage[step, j, 0] = clock - 1
            product_stage[step, j, 1] = max(clock - 1, arrived + 2)
            arrived += 2
        else:
            clock += 1
            product_stage[0, j, 0] = product_stage[0, j, 1] = clock - 1
        for n in chunks:
            x_stage[step, j, n] = clock
    z_bits = [2**bit for bit in range((n_z - 1).bit_length())]
    across = max(clock, 2) + 1
    for n_hop in range(len(z_bits)):
        for step, j, n in x_stage:
            ready = max(x_stage[step, j, n], product_stage[step, j, 1])
            clock = (z_stage[step, j, n, n_hop - 1] if n_hop else max(ready, 2)) + 1
            moves = links(hops_of(step, j)[n_hop])
            while any((clock, link) in busy for link in moves):
                clock += 1
            busy.update((clock, link) for link in moves)
            z_stage[step, j, n, n_hop] = clock
    last = max(*z_stage.values(), across + 1)

    my_start = d * rows_dev
    block = my_start // block_size
    flags = jnp.stack([w * local_blocks, core, x]).astype(jnp.int32)
    env = {"acts": acts, "cotan": cotan}
    done = {}

    def turn(rows, j):
        which = [piece(j, at, flip) for at in range(2) for flip in range(2)]
        other, own, across = turned(rows, which, rows_dev)
        return {("p", j, 0): other, ("p", j, 1): own, ("p", j): across}

    def gathered(part, bits):
        for far in bits:
            other = swap_z(part, far)
            mine_first = jnp.concatenate([part, other], axis=0)
            part = jnp.where(z // far % 2 == 0, mine_first, jnp.concatenate([other, part], axis=0))
        return part

    for stage in range(last + 1):
        if stage:
            keys = sorted(env, key=str)
            env = dict(zip(keys, lax.optimization_barrier(tuple(env[k] for k in keys))))
        joined = {}
        if stage == 0:
            ours, theirs = pick(acts, cotan, block_ids, core)
            joined["acts_sib"] = swap_core(acts)
            env.update(turn(cotan, 0))
            scales = (1.0 / samples, tokens / samples)
            keep, away = terms(flags[1:], ours, swap_core(theirs), block_size, scales)
            away = swap_x(away)
            joined["c", 0] = swap_core(env.pop(("p", 0)))
        if stage == 1:
            for j in range(1, z_per_worker):
                joined.update(turn(env["cotan"], j))
        if stage == 2:
            for j in range(1, z_per_worker):
                env["c", j] = swap_core(env.pop(("p", j)))
        arrivals = {}
        for (step, j, at), when in y_stage.items():
            if when == stage:
                joined["r", step, j, at] = from_worker(env["p", j, at], step)
            if when == stage - 1:
                arrivals[step, j, at] = swap_core(env["r", step, j, at][rows_dev:])
        for (step, j, n), when in x_stage.items():
            if when == stage:
                joined["got", step, j, n] = swap_x(env.pop(("out", step, j, n)))
        for (step, j, n, at), when in z_stage.items():
            if when == stage:
                joined["hop", step, j, n] = hop(env["acc", step, j, n], hops_of(step, j)[at])

        if stage == 1:
            part = env["keep"].reshape(-1, block_size)
            for far in z_bits:
                bit = z // far % 2
                parts = part.reshape(2, -1, block_size)
                there = lax.dynamic_index_in_dim(parts, 1 - bit, 0, keepdims=False)
                part = lax.dynamic_index_in_dim(parts, bit, 0, keepdims=False) + swap_z(there, far)
            joined["keep"] = gathered(part, z_bits[-1:])
        if stage == 2:
            part = gathered(env["keep"], reversed(z_bits[:-1]))
            joined["keep"] = part.reshape(local_blocks, -1, block_size)
        if stage == across:
            joined["back"] = swap_x(env["keep"])
            joined["keep_sib"] = swap_core(env["keep"])
        if stage == across + 1:
            back = env.pop("back")
            *done["factors"], eig_in, eig_local = update_factors(
                flags,
                [env.pop("keep"), back, env.pop("keep_sib"), swap_core(back)],
                (act_factor, grad_factor),
                basis_in,
                basis_out,
            )
            eigs = [eig_local] + [from_worker(eig_local, step) for step in range(1, n_worker)]
            eig_out = jnp.concatenate(eigs, axis=0)
            for key in [key for key in env if key[0] == "acc"]:
                env[key], eig_out = lax.optimization_barrier((env[key], eig_out))

        for (step, j, at), rows in arrivals.items():
            joined["s", step, j, at] = rows
        for step, j in shards:
            due = [at for at in range(2) if product_stage[step, j, at] == stage]
            if due:
                known = {**env, **joined} if stage == 0 else {**env, **{("s", *k): v for k, v in arrivals.items()}}
                if step == 0:
                    halves = [[known["p", j, at] for at in range(2)], [known["c", j]]]
                else:
                    halves = [[known[name, step, j, at] for at in due] for name in ("r", "s")]
                found = products(halves, len(due), rows_dev, (known["acts"], known["acts_sib"]), len(starts))
                for at, outs in zip(due, found):
                    for n in chunks:
                        joined["mine" if at else "out", step, j, n] = outs[n]
        if stage == 0:
            keep, joined["out", 0, 0, 0] = lax.optimization_barrier((keep, joined["out", 0, 0, 0]))
            joined["keep"] = keep + away
        env.update(joined)
        for step, j, n in x_stage:
            mine, got, acc = ("mine", step, j, n), ("got", step, j, n), ("acc", step, j, n)
            if mine in env and got in env:
                env[acc] = env.pop(mine) + env.pop(got)
            if ("hop", step, j, n) in env:
                env[acc] = env[acc] + env.pop(("hop", step, j, n))
        for step, j, n in x_stage:
            if stage == z_stage[step, j, n, len(z_bits) - 1]:
                ends = jnp.array([place((i + step) % n_worker, j) for i in range(n_worker)], jnp.int32)
                acc = env.pop(("acc", step, j, n))
                env["sum", n] = jnp.where(ends[w] == z, acc, env["sum", n]) if ("sum", n) in env else acc

    act_new, grad_new = done["factors"]
    held = (block // local_blocks - w) % n_worker * local_blocks + block % local_blocks

    sharers = block_size // rows_dev
    spot = jnp.stack([block, d % sharers, held]).astype(jnp.int32)
    precond = None
    for n in range(len(starts)):
        parts = [env["sum", n]]
        for step in range(1, sharers):
            pairs = [(i, i // sharers * sharers + (i + step) % sharers) for i in range(n_dp)]
            parts.append(lax.ppermute(parts[0], "dp", pairs))
        precond = tail(spot, parts, basis_in, basis_out, eig_in, eig_out, n, precond)
    return precond, act_new, grad_new


def solution(mesh):
    return jax.shard_map(
        per_device,
        mesh=mesh,
        in_specs=(
            P("dp", "worker"),
            P("dp", "worker"),
            P("dp"),
            P("worker", None, None),
            P(),
            P("worker", None, None),
            P("worker", None, None),
        ),
        out_specs=(P("dp", "worker"), P("worker", None, None), P("worker", None, None)),
        check_vma=False,
    )
```

```python
import functools

import jax
import jax.numpy as jnp
from jax import lax
from jax.experimental import pallas as pl
from jax.experimental.pallas import tpu as pltpu
from jax.sharding import PartitionSpec as P

BLK = 128
QUARTER = 128
VMEM = 56 * 2**20
COL_CHUNKS = 1


DECAY_RATE = 0.75
DAMPING = 0.03

BF16 = jnp.bfloat16
F32 = jnp.float32

SMALL = pl.CostEstimate(flops=1, bytes_accessed=1, transcendentals=0)


def pick_kernel(n_picks, which_ref, acts, cotan, ours, theirs):
    is_act = which_ref[n_picks] == 0
    ours[...] = jnp.where(is_act, acts[...], cotan[...])
    theirs[...] = jnp.where(is_act, cotan[...], acts[...])


def pick(acts, cotan, block_ids, core):
    n_picks, width = block_ids.shape[0], acts.shape[1]
    chosen = pl.BlockSpec((BLK, width), lambda i, which: (which[i], 0))
    out = pl.BlockSpec((BLK, width), lambda i, which: (i, 0))
    return pl.pallas_call(
        functools.partial(pick_kernel, n_picks),
        grid_spec=pltpu.PrefetchScalarGridSpec(
            num_scalar_prefetch=1, grid=(n_picks,), in_specs=[chosen] * 2, out_specs=[out] * 2
        ),
        out_shape=[jax.ShapeDtypeStruct((n_picks * BLK, width), BF16)] * 2,
        compiler_params=pltpu.CompilerParams(vmem_limit_bytes=VMEM),
        cost_estimate=SMALL,
    )(jnp.concatenate([block_ids, jnp.reshape(core, (1,))]).astype(jnp.int32), acts, cotan)


def pack_upper(full):
    q = QUARTER
    second = jnp.concatenate([full[q : 2 * q, q:], full[3 * q :, 3 * q :]], axis=1)
    third = full[2 * q : 3 * q, 2 * q :]
    third = jnp.concatenate([third[: q // 2], third[q // 2 :]], axis=1)
    return jnp.concatenate([full[:q], second, third], axis=0)


def term_kernel(scales, place_ref, ours, theirs, keep, away):
    total = 0.0
    for rows in (ours[...], theirs[...]):
        total = total + lax.dot_general(
            rows, rows, (((0,), (0,)), ((), ())), preferred_element_type=F32
        )
    scale = jnp.where(place_ref[0] == 0, scales[0], scales[1]).astype(F32)
    packed = pack_upper(total * scale)
    half = packed.shape[0] // 2
    low = place_ref[1] == 0
    keep[0] = jnp.where(low, packed[:half], packed[half:]).astype(BF16)
    away[0] = jnp.where(low, packed[half:], packed[:half]).astype(BF16)


def terms(place, ours, theirs, size, scales):
    rows, width = ours.shape
    blocks, half = width // size, 5 * QUARTER // 4
    strip = pl.BlockSpec((rows, size), lambda b, place: (0, b))
    out = pl.BlockSpec((1, half, size), lambda b, place: (b, 0, 0))
    return pl.pallas_call(
        functools.partial(term_kernel, scales),
        grid_spec=pltpu.PrefetchScalarGridSpec(
            num_scalar_prefetch=1, grid=(blocks,), in_specs=[strip] * 2, out_specs=[out] * 2
        ),
        out_shape=[jax.ShapeDtypeStruct((blocks, half, size), BF16)] * 2,
        compiler_params=pltpu.CompilerParams(vmem_limit_bytes=VMEM),
        cost_estimate=SMALL,
    )(place, ours, theirs)


def unpack_upper(packed):
    q = QUARTER
    tiles = {}
    for j in range(4):
        tiles[0, j] = packed[:q, j * q : (j + 1) * q]
    for j in range(1, 4):
        tiles[1, j] = packed[q : 2 * q, (j - 1) * q : j * q]
    tiles[3, 3] = packed[q : 2 * q, 3 * q :]
    third = jnp.concatenate([packed[2 * q :, : 2 * q], packed[2 * q :, 2 * q :]], axis=0)
    tiles[2, 2], tiles[2, 3] = third[:, :q], third[:, q:]
    return [[tiles[i, j] if j >= i else tiles[j, i].T for j in range(4)] for i in range(4)]


def factor_kernel(place_ref, keep, back, keep_sib, back_sib, *refs):
    low = place_ref[2] == 0
    for kind, (factor, basis, new, eig) in enumerate(zip(refs[0:2], refs[2:4], refs[4:6], refs[6:8])):
        here = place_ref[1] == kind
        kept = jnp.where(here, keep[0], keep_sib[0])
        came = jnp.where(here, back[0], back_sib[0])
        halves = [jnp.where(low, kept, came), jnp.where(low, came, kept)]
        rows = unpack_upper(jnp.concatenate(halves, axis=0).astype(F32))
        q = QUARTER
        for i in range(4):
            for j in range(4):
                at = (0, pl.ds(i * q, q), pl.ds(j * q, q))
                new[at] = DECAY_RATE * factor[at] + (1.0 - DECAY_RATE) * rows[i][j]
        vectors = basis[0]
        rest = new[0]
        product = 0.0
        for _ in range(3):
            part = rest.astype(BF16)
            rest = rest - part.astype(F32)
            product = product + jnp.dot(part, vectors, preferred_element_type=F32)
        eig[0] = jnp.sum(vectors.astype(F32) * product, axis=0, keepdims=True)


def update_factors(place, halves, factors, basis_in, basis_out):
    blocks, size, _ = basis_in.shape

    def local(b, place):
        return (b, 0, 0)

    square = pl.BlockSpec((1, size, size), local)
    narrow = pl.BlockSpec((1, halves[0].shape[1], size), local)
    line = pl.BlockSpec((1, 1, size), local)
    return pl.pallas_call(
        factor_kernel,
        grid_spec=pltpu.PrefetchScalarGridSpec(
            num_scalar_prefetch=1,
            grid=(blocks,),
            in_specs=[narrow] * 4
            + [square] * 3
            + [pl.BlockSpec((1, size, size), lambda b, place: (place[0] + b, 0, 0))],
            out_specs=[square, square, line, line],
        ),
        out_shape=[jax.ShapeDtypeStruct((blocks, size, size), F32)] * 2
        + [jax.ShapeDtypeStruct((blocks, 1, size), F32)] * 2,
        compiler_params=pltpu.CompilerParams(vmem_limit_bytes=VMEM),
        cost_estimate=SMALL,
    )(place, *halves, *factors, basis_in, basis_out)


def tail_kernel(n_parts, place_ref, *refs):
    parts, (basis, outer, eig_in, eig_out) = refs[:n_parts], refs[n_parts : n_parts + 4]
    out, whole = refs[-2:]
    sharers = len(parts)
    rows = parts[0].shape[0]
    me = place_ref[1]
    size = whole.shape[1]
    columns = pl.ds(pl.multiple_of(pl.program_id(0) * size, size), size)
    for step, part in enumerate(parts):
        spot = lax.rem(me - step + sharers, sharers)
        whole[pl.ds(pl.multiple_of(spot * rows, rows), rows), :] = part[:, columns]
    right = jnp.dot(whole[...], basis[0], preferred_element_type=F32).astype(BF16)
    inner = lax.dot_general(outer[0], right, (((0,), (0,)), ((), ())), preferred_element_type=F32)
    column = jnp.broadcast_to(eig_out[0], (QUARTER, eig_out.shape[2])).T[:, :1]
    scaled = (inner / (column * eig_in[0] + DAMPING)).astype(BF16)
    mine = outer[0, pl.ds(pl.multiple_of(me * rows, rows), rows), :]
    upper = jnp.dot(mine, scaled, preferred_element_type=F32).astype(BF16)
    out[...] = lax.dot_general(
        upper, basis[0], (((1,), (1,)), ((), ())), preferred_element_type=F32
    ).astype(BF16)


def tail(place, parts, basis_in, basis_out, eig_in, eig_out, chunk, filled):
    blocks, size, _ = basis_in.shape
    rows, cols = parts[0].shape
    each = cols // size
    in_specs = [pl.BlockSpec(memory_space=pltpu.VMEM)] * len(parts) + [
        pl.BlockSpec((1, size, size), lambda b, place: (chunk * each + b, 0, 0)),
        pl.BlockSpec((1, size, size), lambda b, place: (place[0], 0, 0)),
        pl.BlockSpec((1, 1, size), lambda b, place: (chunk * each + b, 0, 0)),
        pl.BlockSpec((1, 1, size), lambda b, place: (place[2], 0, 0)),
    ]
    args = [place, *parts, basis_in, basis_out, eig_in, eig_out]
    aliases = {}
    if filled is not None:
        in_specs.append(pl.BlockSpec(memory_space=pl.ANY))
        aliases = {len(args): 0}
        args.append(filled)
    return pl.pallas_call(
        functools.partial(tail_kernel, len(parts)),
        grid_spec=pltpu.PrefetchScalarGridSpec(
            num_scalar_prefetch=1,
            grid=(each,),
            in_specs=in_specs,
            out_specs=pl.BlockSpec((rows, size), lambda b, place: (0, chunk * each + b)),
            scratch_shapes=[pltpu.VMEM((size, size), BF16)],
        ),
        out_shape=jax.ShapeDtypeStruct((rows, blocks * size), BF16),
        input_output_aliases=aliases,
        compiler_params=pltpu.CompilerParams(vmem_limit_bytes=VMEM),
        cost_estimate=pl.CostEstimate(
            flops=each * 6 * size**3, bytes_accessed=4 * each * size**2, transcendentals=0
        ),
    )(*args)


def turn_kernel(which_ref, block, first, second, across):
    del which_ref
    step = pl.program_id(0)
    flipped = block[...].T

    @pl.when(step < 2)
    def _():
        first[...] = flipped

    @pl.when(step >= 2)
    def _():
        second[...] = flipped

    @pl.when(step % 2 == 1)
    def _():
        across[...] = flipped


def turned(rows, which, n_rows):
    tokens, _ = rows.shape

    def out(place):
        return pl.BlockSpec((n_rows, tokens), lambda i, which: (place(i), 0))

    return pl.pallas_call(
        turn_kernel,
        grid_spec=pltpu.PrefetchScalarGridSpec(
            num_scalar_prefetch=1,
            grid=(4,),
            in_specs=[pl.BlockSpec((tokens, n_rows), lambda i, which: (0, which[i]))],
            out_specs=[
                out(lambda i: jnp.minimum(i, 1)),
                out(lambda i: jnp.maximum(i - 2, 0)),
                out(lambda i: i // 2),
            ],
        ),
        out_shape=[jax.ShapeDtypeStruct((2 * n_rows, tokens), BF16)] * 3,
        compiler_params=pltpu.CompilerParams(vmem_limit_bytes=VMEM),
        cost_estimate=SMALL,
    )(jnp.stack(which).astype(jnp.int32), rows)


def product_kernel(counts, n_outs, *refs):
    n_left = sum(counts)
    halves = refs[: counts[0]], refs[counts[0] : n_left]
    right, outs, left = refs[n_left : n_left + 2], refs[n_left + 2 : -1], refs[-1]
    step = pl.program_id(0)
    tokens = right[0].shape[0]

    @pl.when(step == 0)
    def _():
        for half, pieces in enumerate(halves):
            row = 0
            for piece in pieces:
                left[row : row + piece.shape[0], half * tokens : (half + 1) * tokens] = piece[...]
                row += piece.shape[0]

    total = jnp.dot(left[:, :tokens], right[0][...], preferred_element_type=F32)
    total = total + jnp.dot(left[:, tokens:], right[1][...], preferred_element_type=F32)
    chunks = len(outs) // n_outs
    rows = left.shape[0] // n_outs
    each = pl.num_programs(0) // chunks
    for n in range(chunks):

        @pl.when(step // each == n)
        def _(n=n):
            for at in range(n_outs):
                outs[at * chunks + n][...] = total[at * rows : (at + 1) * rows].astype(BF16)


def products(halves, n_outs, n_rows, rows, chunks):
    tokens, width = rows[0].shape
    tile = 512
    each = width // chunks // tile
    strip = pl.BlockSpec((tokens, tile), lambda i: (0, i))
    first, second = ([min(p.shape[0], n_rows * n_outs // len(half)) for p in half] for half in halves)
    outs = pl.pallas_call(
        functools.partial(product_kernel, [len(half) for half in halves], n_outs),
        grid=(width // tile,),
        in_specs=[pl.BlockSpec((size, tokens), lambda i: (0, 0)) for size in first + second] + [strip] * 2,
        out_specs=[
            pl.BlockSpec((n_rows, tile), lambda i, n=n: (0, jnp.clip(i - n * each, 0, each - 1)))
            for _ in range(n_outs)
            for n in range(chunks)
        ],
        out_shape=[jax.ShapeDtypeStruct((n_rows, width // chunks), BF16)] * (n_outs * chunks),
        scratch_shapes=[pltpu.VMEM((n_outs * n_rows, 2 * tokens), BF16)],
        compiler_params=pltpu.CompilerParams(vmem_limit_bytes=VMEM),
        cost_estimate=pl.CostEstimate(
            flops=8 * n_outs * tokens * n_rows * width, bytes_accessed=4 * tokens * width, transcendentals=0
        ),
    )(*halves[0], *halves[1], *rows)
    return [outs[m * chunks : (m + 1) * chunks] for m in range(n_outs)]


def per_device(acts, cotan, block_ids, basis_in, basis_out, act_factor, grad_factor):
    n_dp = lax.axis_size("dp")
    n_worker = lax.axis_size("worker")
    d = lax.axis_index("dp")
    w = lax.axis_index("worker")
    core, x = d % 2, (d // 2) % 2
    n_z = n_dp // 4
    pool_rows, width = acts.shape
    local_blocks, block_size, _ = basis_in.shape
    model_width = basis_out.shape[0] * block_size
    samples = block_ids.shape[0] * BLK * n_dp
    tokens = pool_rows * n_dp
    rows_dev = model_width // n_dp
    z_per_worker = n_z // n_worker
    cols = width // COL_CHUNKS
    both = ("dp", "worker")

    def swap_core(v):
        return lax.ppermute(v, "dp", [(i, i ^ 1) for i in range(n_dp)])

    def swap_x(v):
        return lax.ppermute(v, "dp", [(i, i ^ 2) for i in range(n_dp)])

    def from_worker(v, step):
        return lax.ppermute(v, "worker", [((j + step) % n_worker, j) for j in range(n_worker)])

    def place(owner, j):
        return owner * z_per_worker + (j if owner < n_worker // 2 else z_per_worker - 1 - j)

    z = d // 4
    starts = list(range(0, width, cols))
    shards = [(step, j) for j in range(z_per_worker) for step in range(n_worker)]

    def hops_of(step, j):
        hops = []
        size = 1
        while size < n_z:
            moves = []
            for i in range(n_worker):
                end = place((i + step) % n_worker, j)
                for low in range(0, n_z, 2 * size):
                    heads = [min(max(end, at), at + size - 1) for at in (low, low + size)]
                    to = min(max(end, low), low + 2 * size - 1)
                    moves.append((i, sum(heads) - to, to))
            hops.append(moves)
            size *= 2
        return hops

    def links(moves):
        found = set()
        for i, a, b in moves:
            ahead = 1 if b > a else -1
            found.update((i, at, at + ahead) for at in range(a, b, ahead))
        return found

    def swap_z(v, bit):
        return lax.ppermute(v, "dp", [(i, i ^ (4 * bit)) for i in range(n_dp)])

    def hop(v, moves):
        pairs = [((a * 4 + r) * n_worker + i, (b * 4 + r) * n_worker + i) for i, a, b in moves for r in range(4)]
        return lax.ppermute(v, both, pairs)

    def piece(j, at, flip):
        part = jnp.where(w < n_worker // 2, j, z_per_worker - 1 - j)
        x_to = x if at else 1 - x
        core_to = 1 - core if flip else core
        return (part * 2 + x_to) * 2 + core_to

    chunks = range(len(starts))
    x_stage, y_stage, z_stage, product_stage, busy = {}, {}, {}, {}, set()
    clock = arrived = 0
    for step, j in shards:
        if step:
            for at in range(2):
                y_stage[step, j, at] = arrived + at
            clock = max(clock + 1, arrived + 2)
            product_stage[step, j, 0] = clock - 1
            product_stage[step, j, 1] = max(clock - 1, arrived + 2)
            arrived += 2
        else:
            clock += 1
            product_stage[0, j, 0] = product_stage[0, j, 1] = clock - 1
        for n in chunks:
            x_stage[step, j, n] = clock
    z_bits = [2**bit for bit in range((n_z - 1).bit_length())]
    across = max(clock, 2) + 1
    for n_hop in range(len(z_bits)):
        for step, j, n in x_stage:
            ready = max(x_stage[step, j, n], product_stage[step, j, 1])
            clock = (z_stage[step, j, n, n_hop - 1] if n_hop else max(ready, 2)) + 1
            moves = links(hops_of(step, j)[n_hop])
            while any((clock, link) in busy for link in moves):
                clock += 1
            busy.update((clock, link) for link in moves)
            z_stage[step, j, n, n_hop] = clock
    last = max(*z_stage.values(), across + 1)

    my_start = d * rows_dev
    block = my_start // block_size
    flags = jnp.stack([w * local_blocks, core, x]).astype(jnp.int32)
    env = {"acts": acts, "cotan": cotan}
    done = {}

    def turn(rows, j):
        which = [piece(j, at, flip) for at in range(2) for flip in range(2)]
        other, own, across = turned(rows, which, rows_dev)
        return {("p", j, 0): other, ("p", j, 1): own, ("p", j): across}

    def gathered(part, bits, tie=lambda v: v):
        for far in bits:
            other = tie(swap_z(part, far))
            mine_first = jnp.concatenate([part, other], axis=0)
            part = jnp.where(z // far % 2 == 0, mine_first, jnp.concatenate([other, part], axis=0))
        return part

    for stage in range(last + 1):
        if stage:
            keys = sorted(env, key=str)
            env = dict(zip(keys, lax.optimization_barrier(tuple(env[k] for k in keys))))
        joined = {}
        if stage == 0:
            ours, theirs = pick(acts, cotan, block_ids, core)
            joined["acts_sib"] = swap_core(acts)
            env.update(turn(cotan, 0))
            scales = (1.0 / samples, tokens / samples)
            keep, away = terms(flags[1:], ours, swap_core(theirs), block_size, scales)
            away = swap_x(away)
            joined["c", 0] = swap_core(env.pop(("p", 0)))
        if stage == 1:
            for j in range(1, z_per_worker):
                joined.update(turn(env["cotan"], j))
        if stage == 2:
            for j in range(1, z_per_worker):
                env["c", j] = swap_core(env.pop(("p", j)))
        arrivals = {}
        for (step, j, at), when in y_stage.items():
            if when == stage:
                joined["r", step, j, at] = from_worker(env["p", j, at], step)
            if when == stage - 1:
                arrivals[step, j, at] = swap_core(env["r", step, j, at][rows_dev:])
        for (step, j, n), when in x_stage.items():
            if when == stage:
                joined["got", step, j, n] = swap_x(env.pop(("out", step, j, n)))
        for (step, j, n, at), when in z_stage.items():
            if when == stage:
                joined["hop", step, j, n] = hop(env["acc", step, j, n], hops_of(step, j)[at])

        if stage == 1:
            part = env["keep"].reshape(-1, block_size)
            for far in z_bits:
                bit = z // far % 2
                parts = part.reshape(2, -1, block_size)
                there = lax.dynamic_index_in_dim(parts, 1 - bit, 0, keepdims=False)
                part = lax.dynamic_index_in_dim(parts, bit, 0, keepdims=False) + swap_z(there, far)
            joined["keep"] = gathered(part, z_bits[-1:])
        if stage == across:
            joined["back"] = swap_x(env["keep"])
            joined["keep_sib"] = swap_core(env["keep"])
        if stage == across + 1:
            back = env.pop("back")
            *done["factors"], eig_in, eig_local = update_factors(
                flags,
                [env.pop("keep"), back, env.pop("keep_sib"), swap_core(back)],
                (act_factor, grad_factor),
                basis_in,
                basis_out,
            )
            eigs = [eig_local] + [from_worker(eig_local, step) for step in range(1, n_worker)]
            eig_out = jnp.concatenate(eigs, axis=0)
            for key in [key for key in env if key[0] == "acc"]:
                env[key], eig_out = lax.optimization_barrier((env[key], eig_out))

        for (step, j, at), rows in arrivals.items():
            joined["s", step, j, at] = rows
        for step, j in shards:
            due = [at for at in range(2) if product_stage[step, j, at] == stage]
            if due:
                known = {**env, **joined} if stage == 0 else {**env, **{("s", *k): v for k, v in arrivals.items()}}
                if step == 0:
                    halves = [[known["p", j, at] for at in range(2)], [known["c", j]]]
                else:
                    halves = [[known[name, step, j, at] for at in due] for name in ("r", "s")]
                found = products(halves, len(due), rows_dev, (known["acts"], known["acts_sib"]), len(starts))
                for at, outs in zip(due, found):
                    for n in chunks:
                        joined["mine" if at else "out", step, j, n] = outs[n]
        made = [value for key, value in joined.items() if key[0] in ("out", "mine")]

        def behind(v, made=made):
            return lax.optimization_barrier((v, *made))[0] if made else v

        if stage == 2:
            part = gathered(env["keep"], reversed(z_bits[:-1]), behind)
            joined["keep"] = part.reshape(local_blocks, -1, block_size)
        if stage == 0:
            keep, joined["out", 0, 0, 0] = lax.optimization_barrier((keep, joined["out", 0, 0, 0]))
            joined["keep"] = keep + away
        env.update(joined)
        for step, j, n in x_stage:
            mine, got, acc = ("mine", step, j, n), ("got", step, j, n), ("acc", step, j, n)
            if mine in env and got in env:
                env[acc] = behind(env.pop(mine)) + env.pop(got)
            if ("hop", step, j, n) in env:
                env[acc] = behind(env[acc]) + env.pop(("hop", step, j, n))
        for step, j, n in x_stage:
            if stage == z_stage[step, j, n, len(z_bits) - 1]:
                ends = jnp.array([place((i + step) % n_worker, j) for i in range(n_worker)], jnp.int32)
                acc = env.pop(("acc", step, j, n))
                env["sum", n] = jnp.where(ends[w] == z, acc, env["sum", n]) if ("sum", n) in env else acc

    act_new, grad_new = done["factors"]
    held = (block // local_blocks - w) % n_worker * local_blocks + block % local_blocks

    sharers = block_size // rows_dev
    spot = jnp.stack([block, d % sharers, held]).astype(jnp.int32)
    precond = None
    for n in range(len(starts)):
        parts = [env["sum", n]]
        for step in range(1, sharers):
            pairs = [(i, i // sharers * sharers + (i + step) % sharers) for i in range(n_dp)]
            parts.append(lax.ppermute(parts[0], "dp", pairs))
        precond = tail(spot, parts, basis_in, basis_out, eig_in, eig_out, n, precond)
    return precond, act_new, grad_new


def solution(mesh):
    return jax.shard_map(
        per_device,
        mesh=mesh,
        in_specs=(
            P("dp", "worker"),
            P("dp", "worker"),
            P("dp"),
            P("worker", None, None),
            P(),
            P("worker", None, None),
            P("worker", None, None),
        ),
        out_specs=(P("dp", "worker"), P("worker", None, None), P("worker", None, None)),
        check_vma=False,
    )
```

```python
import functools

import jax
import jax.numpy as jnp
from jax import lax
from jax.experimental import pallas as pl
from jax.experimental.pallas import tpu as pltpu
from jax.sharding import PartitionSpec as P

BLK = 128
QUARTER = 128
VMEM = 56 * 2**20
COL_CHUNKS = 1


DECAY_RATE = 0.75
DAMPING = 0.03

BF16 = jnp.bfloat16
F32 = jnp.float32

SMALL = pl.CostEstimate(flops=1, bytes_accessed=1, transcendentals=0)


def pick_kernel(ids_ref, place_ref, acts, cotan, ours, theirs):
    del ids_ref
    is_act = place_ref[1] == 0
    ours[...] = jnp.where(is_act, acts[...], cotan[...])
    theirs[...] = jnp.where(is_act, cotan[...], acts[...])


def pick(acts, cotan, block_ids, place):
    n_picks, width = block_ids.shape[0], acts.shape[1]
    chosen = pl.BlockSpec((BLK, width), lambda i, ids, place: (ids[i], 0))
    out = pl.BlockSpec((BLK, width), lambda i, ids, place: (i, 0))
    return pl.pallas_call(
        pick_kernel,
        grid_spec=pltpu.PrefetchScalarGridSpec(
            num_scalar_prefetch=2, grid=(n_picks,), in_specs=[chosen] * 2, out_specs=[out] * 2
        ),
        out_shape=[jax.ShapeDtypeStruct((n_picks * BLK, width), BF16)] * 2,
        compiler_params=pltpu.CompilerParams(vmem_limit_bytes=VMEM),
        cost_estimate=SMALL,
    )(block_ids, place, acts, cotan)


def pack_upper(full):
    q = QUARTER
    second = jnp.concatenate([full[q : 2 * q, q:], full[3 * q :, 3 * q :]], axis=1)
    third = full[2 * q : 3 * q, 2 * q :]
    third = jnp.concatenate([third[: q // 2], third[q // 2 :]], axis=1)
    return jnp.concatenate([full[:q], second, third], axis=0)


def term_kernel(scales, place_ref, ours, theirs, keep, away):
    total = 0.0
    for rows in (ours[...], theirs[...]):
        total = total + lax.dot_general(
            rows, rows, (((0,), (0,)), ((), ())), preferred_element_type=F32
        )
    scale = jnp.where(place_ref[1] == 0, scales[0], scales[1]).astype(F32)
    packed = pack_upper(total * scale)
    half = packed.shape[0] // 2
    low = place_ref[2] == 0
    keep[0] = jnp.where(low, packed[:half], packed[half:]).astype(BF16)
    away[0] = jnp.where(low, packed[half:], packed[:half]).astype(BF16)


def terms(place, ours, theirs, size, scales):
    rows, width = ours.shape
    blocks, half = width // size, 5 * QUARTER // 4
    strip = pl.BlockSpec((rows, size), lambda b, place: (0, b))
    out = pl.BlockSpec((1, half, size), lambda b, place: (b, 0, 0))
    return pl.pallas_call(
        functools.partial(term_kernel, scales),
        grid_spec=pltpu.PrefetchScalarGridSpec(
            num_scalar_prefetch=1, grid=(blocks,), in_specs=[strip] * 2, out_specs=[out] * 2
        ),
        out_shape=[jax.ShapeDtypeStruct((blocks, half, size), BF16)] * 2,
        compiler_params=pltpu.CompilerParams(vmem_limit_bytes=VMEM),
        cost_estimate=SMALL,
    )(place, ours, theirs)


def unpack_upper(packed):
    q = QUARTER
    tiles = {}
    for j in range(4):
        tiles[0, j] = packed[:q, j * q : (j + 1) * q]
    for j in range(1, 4):
        tiles[1, j] = packed[q : 2 * q, (j - 1) * q : j * q]
    tiles[3, 3] = packed[q : 2 * q, 3 * q :]
    third = jnp.concatenate([packed[2 * q :, : 2 * q], packed[2 * q :, 2 * q :]], axis=0)
    tiles[2, 2], tiles[2, 3] = third[:, :q], third[:, q:]
    return [[tiles[i, j] if j >= i else tiles[j, i].T for j in range(4)] for i in range(4)]


def factor_kernel(place_ref, keep, back, keep_sib, back_sib, *refs):
    low = place_ref[2] == 0
    for kind, (factor, basis, new, eig) in enumerate(zip(refs[0:2], refs[2:4], refs[4:6], refs[6:8])):
        here = place_ref[1] == kind
        kept = jnp.where(here, keep[0], keep_sib[0])
        came = jnp.where(here, back[0], back_sib[0])
        halves = [jnp.where(low, kept, came), jnp.where(low, came, kept)]
        rows = unpack_upper(jnp.concatenate(halves, axis=0).astype(F32))
        q = QUARTER
        for i in range(4):
            for j in range(4):
                at = (0, pl.ds(i * q, q), pl.ds(j * q, q))
                new[at] = DECAY_RATE * factor[at] + (1.0 - DECAY_RATE) * rows[i][j]
        vectors = basis[0]
        rest = new[0]
        product = 0.0
        for _ in range(3):
            part = rest.astype(BF16)
            rest = rest - part.astype(F32)
            product = product + jnp.dot(part, vectors, preferred_element_type=F32)
        eig[0] = jnp.sum(vectors.astype(F32) * product, axis=0, keepdims=True)


def update_factors(place, halves, factors, basis_in, basis_out):
    blocks, size, _ = basis_in.shape

    def local(b, place):
        return (b, 0, 0)

    square = pl.BlockSpec((1, size, size), local)
    narrow = pl.BlockSpec((1, halves[0].shape[1], size), local)
    line = pl.BlockSpec((1, 1, size), local)
    return pl.pallas_call(
        factor_kernel,
        grid_spec=pltpu.PrefetchScalarGridSpec(
            num_scalar_prefetch=1,
            grid=(blocks,),
            in_specs=[narrow] * 4
            + [square] * 3
            + [pl.BlockSpec((1, size, size), lambda b, place: (place[0] + b, 0, 0))],
            out_specs=[square, square, line, line],
        ),
        out_shape=[jax.ShapeDtypeStruct((blocks, size, size), F32)] * 2
        + [jax.ShapeDtypeStruct((blocks, 1, size), F32)] * 2,
        compiler_params=pltpu.CompilerParams(vmem_limit_bytes=VMEM),
        cost_estimate=SMALL,
    )(place, *halves, *factors, basis_in, basis_out)


def tail_kernel(n_parts, place_ref, *refs):
    parts, (basis, outer, eig_in, eig_out) = refs[:n_parts], refs[n_parts : n_parts + 4]
    out, whole, flipped = refs[-3:]
    sharers = len(parts)
    rows = parts[0].shape[0]
    me = place_ref[4]
    size = whole.shape[1]
    columns = pl.ds(pl.multiple_of(pl.program_id(0) * size, size), size)
    for step, part in enumerate(parts):
        spot = lax.rem(me - step + sharers, sharers)
        whole[pl.ds(pl.multiple_of(spot * rows, rows), rows), :] = part[:, columns]
    right = jnp.dot(whole[...], basis[0], preferred_element_type=F32).astype(BF16)

    @pl.when(pl.program_id(0) == 0)
    def _():
        flipped[...] = outer[0].T

    inner = jnp.dot(flipped[...], right, preferred_element_type=F32)
    column = jnp.broadcast_to(eig_out[0], (QUARTER, eig_out.shape[2])).T[:, :1]
    scaled = (inner / (column * eig_in[0] + DAMPING)).astype(BF16)
    mine = outer[0, pl.ds(pl.multiple_of(me * rows, rows), rows), :]
    upper = jnp.dot(mine, scaled, preferred_element_type=F32).astype(BF16)
    out[...] = lax.dot_general(
        upper, basis[0], (((1,), (1,)), ((), ())), preferred_element_type=F32
    ).astype(BF16)


def tail(place, parts, basis_in, basis_out, eig_in, eig_out, chunk, filled):
    blocks, size, _ = basis_in.shape
    rows, cols = parts[0].shape
    each = cols // size
    in_specs = [pl.BlockSpec(memory_space=pltpu.VMEM)] * len(parts) + [
        pl.BlockSpec((1, size, size), lambda b, place: (chunk * each + b, 0, 0)),
        pl.BlockSpec((1, size, size), lambda b, place: (place[3], 0, 0)),
        pl.BlockSpec((1, 1, size), lambda b, place: (chunk * each + b, 0, 0)),
        pl.BlockSpec((1, 1, size), lambda b, place: (place[5], 0, 0)),
    ]
    args = [place, *parts, basis_in, basis_out, eig_in, eig_out]
    aliases = {}
    if filled is not None:
        in_specs.append(pl.BlockSpec(memory_space=pl.ANY))
        aliases = {len(args): 0}
        args.append(filled)
    return pl.pallas_call(
        functools.partial(tail_kernel, len(parts)),
        grid_spec=pltpu.PrefetchScalarGridSpec(
            num_scalar_prefetch=1,
            grid=(each,),
            in_specs=in_specs,
            out_specs=pl.BlockSpec((rows, size), lambda b, place: (0, chunk * each + b)),
            scratch_shapes=[pltpu.VMEM((size, size), BF16)] * 2,
        ),
        out_shape=jax.ShapeDtypeStruct((rows, blocks * size), BF16),
        input_output_aliases=aliases,
        compiler_params=pltpu.CompilerParams(vmem_limit_bytes=VMEM),
        cost_estimate=pl.CostEstimate(
            flops=each * 6 * size**3, bytes_accessed=4 * each * size**2, transcendentals=0
        ),
    )(*args)


def turn_kernel(which_ref, block, first, second, across):
    del which_ref
    step = pl.program_id(0)
    flipped = block[...].T

    @pl.when(step < 2)
    def _():
        first[...] = flipped

    @pl.when(step >= 2)
    def _():
        second[...] = flipped

    @pl.when(step % 2 == 1)
    def _():
        across[...] = flipped


def turned(rows, place, first_piece, n_rows):
    tokens, _ = rows.shape

    def out(spot):
        return pl.BlockSpec((n_rows, tokens), lambda i, place: (spot(i), 0))

    return pl.pallas_call(
        turn_kernel,
        grid_spec=pltpu.PrefetchScalarGridSpec(
            num_scalar_prefetch=1,
            grid=(4,),
            in_specs=[pl.BlockSpec((tokens, n_rows), lambda i, place: (0, place[first_piece + i]))],
            out_specs=[
                out(lambda i: jnp.minimum(i, 1)),
                out(lambda i: jnp.maximum(i - 2, 0)),
                out(lambda i: i // 2),
            ],
        ),
        out_shape=[jax.ShapeDtypeStruct((2 * n_rows, tokens), BF16)] * 3,
        compiler_params=pltpu.CompilerParams(vmem_limit_bytes=VMEM),
        cost_estimate=SMALL,
    )(place, rows)


def product_kernel(counts, n_outs, *refs):
    n_left = sum(counts)
    halves = refs[: counts[0]], refs[counts[0] : n_left]
    right, outs, left = refs[n_left : n_left + 2], refs[n_left + 2 : -1], refs[-1]
    step = pl.program_id(0)
    tokens = right[0].shape[0]

    @pl.when(step == 0)
    def _():
        for half, pieces in enumerate(halves):
            row = 0
            for piece in pieces:
                left[row : row + piece.shape[0], half * tokens : (half + 1) * tokens] = piece[...]
                row += piece.shape[0]

    total = jnp.dot(left[:, :tokens], right[0][...], preferred_element_type=F32)
    total = total + jnp.dot(left[:, tokens:], right[1][...], preferred_element_type=F32)
    chunks = len(outs) // n_outs
    rows = left.shape[0] // n_outs
    each = pl.num_programs(0) // chunks
    for n in range(chunks):

        @pl.when(step // each == n)
        def _(n=n):
            for at in range(n_outs):
                outs[at * chunks + n][...] = total[at * rows : (at + 1) * rows].astype(BF16)


def products(halves, n_outs, n_rows, rows, chunks):
    tokens, width = rows[0].shape
    tile = 512
    each = width // chunks // tile
    strip = pl.BlockSpec((tokens, tile), lambda i: (0, i))
    first, second = ([min(p.shape[0], n_rows * n_outs // len(half)) for p in half] for half in halves)
    outs = pl.pallas_call(
        functools.partial(product_kernel, [len(half) for half in halves], n_outs),
        grid=(width // tile,),
        in_specs=[pl.BlockSpec((size, tokens), lambda i: (0, 0)) for size in first + second] + [strip] * 2,
        out_specs=[
            pl.BlockSpec((n_rows, tile), lambda i, n=n: (0, jnp.clip(i - n * each, 0, each - 1)))
            for _ in range(n_outs)
            for n in range(chunks)
        ],
        out_shape=[jax.ShapeDtypeStruct((n_rows, width // chunks), BF16)] * (n_outs * chunks),
        scratch_shapes=[pltpu.VMEM((n_outs * n_rows, 2 * tokens), BF16)],
        compiler_params=pltpu.CompilerParams(vmem_limit_bytes=VMEM),
        cost_estimate=pl.CostEstimate(
            flops=8 * n_outs * tokens * n_rows * width, bytes_accessed=4 * tokens * width, transcendentals=0
        ),
    )(*halves[0], *halves[1], *rows)
    return [outs[m * chunks : (m + 1) * chunks] for m in range(n_outs)]


def per_device(acts, cotan, block_ids, basis_in, basis_out, act_factor, grad_factor):
    n_dp = lax.axis_size("dp")
    n_worker = lax.axis_size("worker")
    d = lax.axis_index("dp")
    w = lax.axis_index("worker")
    core, x = d % 2, (d // 2) % 2
    n_z = n_dp // 4
    pool_rows, width = acts.shape
    local_blocks, block_size, _ = basis_in.shape
    model_width = basis_out.shape[0] * block_size
    samples = block_ids.shape[0] * BLK * n_dp
    tokens = pool_rows * n_dp
    rows_dev = model_width // n_dp
    z_per_worker = n_z // n_worker
    cols = width // COL_CHUNKS
    both = ("dp", "worker")

    def swap_core(v):
        return lax.ppermute(v, "dp", [(i, i ^ 1) for i in range(n_dp)])

    def swap_x(v):
        return lax.ppermute(v, "dp", [(i, i ^ 2) for i in range(n_dp)])

    def from_worker(v, step):
        return lax.ppermute(v, "worker", [((j + step) % n_worker, j) for j in range(n_worker)])

    def place(owner, j):
        return owner * z_per_worker + (j if owner < n_worker // 2 else z_per_worker - 1 - j)

    z = d // 4
    starts = list(range(0, width, cols))
    shards = [(step, j) for j in range(z_per_worker) for step in range(n_worker)]

    def hops_of(step, j):
        hops = []
        size = 1
        while size < n_z:
            moves = []
            for i in range(n_worker):
                end = place((i + step) % n_worker, j)
                for low in range(0, n_z, 2 * size):
                    heads = [min(max(end, at), at + size - 1) for at in (low, low + size)]
                    to = min(max(end, low), low + 2 * size - 1)
                    moves.append((i, sum(heads) - to, to))
            hops.append(moves)
            size *= 2
        return hops

    def links(moves):
        found = set()
        for i, a, b in moves:
            ahead = 1 if b > a else -1
            found.update((i, at, at + ahead) for at in range(a, b, ahead))
        return found

    def swap_z(v, bit):
        return lax.ppermute(v, "dp", [(i, i ^ (4 * bit)) for i in range(n_dp)])

    def hop(v, moves):
        pairs = [((a * 4 + r) * n_worker + i, (b * 4 + r) * n_worker + i) for i, a, b in moves for r in range(4)]
        return lax.ppermute(v, both, pairs)

    def piece(j, at, flip):
        part = jnp.where(w < n_worker // 2, j, z_per_worker - 1 - j)
        x_to = x if at else 1 - x
        core_to = 1 - core if flip else core
        return (part * 2 + x_to) * 2 + core_to

    chunks = range(len(starts))
    x_stage, y_stage, z_stage, product_stage, busy = {}, {}, {}, {}, set()
    clock = arrived = 0
    for step, j in shards:
        if step:
            for at in range(2):
                y_stage[step, j, at] = arrived + at
            clock = max(clock + 1, arrived + 2)
            product_stage[step, j, 0] = clock - 1
            product_stage[step, j, 1] = max(clock - 1, arrived + 2)
            arrived += 2
        else:
            clock += 1
            product_stage[0, j, 0] = product_stage[0, j, 1] = clock - 1
        for n in chunks:
            x_stage[step, j, n] = clock
    z_bits = [2**bit for bit in range((n_z - 1).bit_length())]
    across = max(clock, 2) + 1
    for n_hop in range(len(z_bits)):
        for step, j, n in x_stage:
            ready = max(x_stage[step, j, n], product_stage[step, j, 1])
            clock = (z_stage[step, j, n, n_hop - 1] if n_hop else max(ready, 2)) + 1
            moves = links(hops_of(step, j)[n_hop])
            while any((clock, link) in busy for link in moves):
                clock += 1
            busy.update((clock, link) for link in moves)
            z_stage[step, j, n, n_hop] = clock
    last = max(*z_stage.values(), across + 1)

    my_start = d * rows_dev
    block = my_start // block_size
    sharers = block_size // rows_dev
    held = (block // local_blocks - w) % n_worker * local_blocks + block % local_blocks
    scalars = [w * local_blocks, core, x, block, d % sharers, held]
    first_piece = len(scalars)
    scalars += [piece(j, at, flip) for j in range(z_per_worker) for at in range(2) for flip in range(2)]
    flags = jnp.stack(scalars).astype(jnp.int32)
    env = {"acts": acts, "cotan": cotan}
    done = {}

    def turn(rows, j):
        other, own, across = turned(rows, flags, first_piece + 4 * j, rows_dev)
        return {("p", j, 0): other, ("p", j, 1): own, ("p", j): across}

    def gathered(part, bits, tie=lambda v: v):
        for far in bits:
            other = tie(swap_z(part, far))
            mine_first = jnp.concatenate([part, other], axis=0)
            part = jnp.where(z // far % 2 == 0, mine_first, jnp.concatenate([other, part], axis=0))
        return part

    for stage in range(last + 1):
        if stage:
            keys = sorted(env, key=str)
            env = dict(zip(keys, lax.optimization_barrier(tuple(env[k] for k in keys))))
        joined = {}
        if stage == 0:
            ours, theirs = pick(acts, cotan, block_ids, flags)
            joined["acts_sib"] = swap_core(acts)
            env.update(turn(cotan, 0))
            scales = (1.0 / samples, tokens / samples)
            keep, away = terms(flags, ours, swap_core(theirs), block_size, scales)
            away = swap_x(away)
            joined["c", 0] = swap_core(env.pop(("p", 0)))
        if stage == 1:
            for j in range(1, z_per_worker):
                joined.update(turn(env["cotan"], j))
        if stage == 2:
            for j in range(1, z_per_worker):
                env["c", j] = swap_core(env.pop(("p", j)))
        arrivals = {}
        for (step, j, at), when in y_stage.items():
            if when == stage:
                joined["r", step, j, at] = from_worker(env["p", j, at], step)
            if when == stage - 1:
                arrivals[step, j, at] = swap_core(env["r", step, j, at][rows_dev:])
        for (step, j, n), when in x_stage.items():
            if when == stage:
                joined["got", step, j, n] = swap_x(env.pop(("out", step, j, n)))
        for (step, j, n, at), when in z_stage.items():
            if when == stage:
                joined["hop", step, j, n] = hop(env["acc", step, j, n], hops_of(step, j)[at])

        if stage == 1:
            part = env["keep"].reshape(-1, block_size)
            for far in z_bits:
                bit = z // far % 2
                parts = part.reshape(2, -1, block_size)
                there = lax.dynamic_index_in_dim(parts, 1 - bit, 0, keepdims=False)
                part = lax.dynamic_index_in_dim(parts, bit, 0, keepdims=False) + swap_z(there, far)
            joined["keep"] = gathered(part, z_bits[-1:])
        if stage == across:
            joined["back"] = swap_x(env["keep"])
            joined["keep_sib"] = swap_core(env["keep"])
        if stage == across + 1:
            back = env.pop("back")
            *done["factors"], eig_in, eig_local = update_factors(
                flags,
                [env.pop("keep"), back, env.pop("keep_sib"), swap_core(back)],
                (act_factor, grad_factor),
                basis_in,
                basis_out,
            )
            eigs = [eig_local] + [from_worker(eig_local, step) for step in range(1, n_worker)]
            eig_out = jnp.concatenate(eigs, axis=0)
            for key in [key for key in env if key[0] == "acc"]:
                env[key], eig_out = lax.optimization_barrier((env[key], eig_out))

        for (step, j, at), rows in arrivals.items():
            joined["s", step, j, at] = rows
        for step, j in shards:
            due = [at for at in range(2) if product_stage[step, j, at] == stage]
            if due:
                known = {**env, **joined} if stage == 0 else {**env, **{("s", *k): v for k, v in arrivals.items()}}
                if step == 0:
                    halves = [[known["p", j, at] for at in range(2)], [known["c", j]]]
                else:
                    halves = [[known[name, step, j, at] for at in due] for name in ("r", "s")]
                found = products(halves, len(due), rows_dev, (known["acts"], known["acts_sib"]), len(starts))
                for at, outs in zip(due, found):
                    for n in chunks:
                        joined["mine" if at else "out", step, j, n] = outs[n]
        made = [value for key, value in joined.items() if key[0] in ("out", "mine")]

        def behind(v, made=made):
            return lax.optimization_barrier((v, *made))[0] if made else v

        if stage == 2:
            part = gathered(env["keep"], reversed(z_bits[:-1]), behind)
            joined["keep"] = part.reshape(local_blocks, -1, block_size)
        if stage == 0:
            keep, joined["out", 0, 0, 0] = lax.optimization_barrier((keep, joined["out", 0, 0, 0]))
            joined["keep"] = keep + away
        env.update(joined)
        for step, j, n in x_stage:
            mine, got, acc = ("mine", step, j, n), ("got", step, j, n), ("acc", step, j, n)
            if mine in env and got in env:
                env[acc] = behind(env.pop(mine)) + env.pop(got)
            if ("hop", step, j, n) in env:
                env[acc] = behind(env[acc]) + env.pop(("hop", step, j, n))
        for step, j, n in x_stage:
            if stage == z_stage[step, j, n, len(z_bits) - 1]:
                ends = jnp.array([place((i + step) % n_worker, j) for i in range(n_worker)], jnp.int32)
                acc = env.pop(("acc", step, j, n))
                env["sum", n] = jnp.where(ends[w] == z, acc, env["sum", n]) if ("sum", n) in env else acc

    act_new, grad_new = done["factors"]

    precond = None
    for n in range(len(starts)):
        parts = [env["sum", n]]
        for step in range(1, sharers):
            pairs = [(i, i // sharers * sharers + (i + step) % sharers) for i in range(n_dp)]
            parts.append(lax.ppermute(parts[0], "dp", pairs))
        precond = tail(flags, parts, basis_in, basis_out, eig_in, eig_out, n, precond)
    return precond, act_new, grad_new


def solution(mesh):
    return jax.shard_map(
        per_device,
        mesh=mesh,
        in_specs=(
            P("dp", "worker"),
            P("dp", "worker"),
            P("dp"),
            P("worker", None, None),
            P(),
            P("worker", None, None),
            P("worker", None, None),
        ),
        out_specs=(P("dp", "worker"), P("worker", None, None), P("worker", None, None)),
        check_vma=False,
    )
```
